512 devices in a mesh: row: 64 (over x, z), col: 8 (over y, core).
Axes of the slice: x: 4, y: 4, z: 16, core: 2. Of those that a mesh axis runs over, the one named last changes fastest.
Arguments:
- matrix: float32 [131072, 1024], P('row', 'col'), may hold values from -90 to 90, as said below
- row_signs: int32 [131072], P('row'), may hold values from -1 to 1, as said below
- sample_block: int32 [16384, 1], P('row'), may hold values from 0 to 63; in each aligned block of 256 rows (0 to 255, 256 to 511, ...) at most 8 rows name the same one
- sample_offset: int32 [16384], P('row'), may hold values from 0 to 2047
Outputs:
- sketch: float32 [16384, 1024], P('row', 'col')
- factor: float32 [1024, 1024], P(None, 'col')
The draws below stay inside these ranges and needn't reach their ends.
Inputs may be any that keep to these rules, and one draw needn't show every extreme that they name: `matrix`: entries are real and of both signs; no structure is promised. `row_signs`: each entry is -1 or 1. `sample_block`: among the 256 samples of one device (aligned blocks) no value is named more than 8 times, a bound that some block reaches.
All inputs are finite; a program needn't handle non-finite values.
Results may differ from the reference program's by a relative error of at most 0.00007.
Values sent between devices are 32-bit elements; how exact they have to be, the bound alone decides.
A program may use at most 64 MiB of HBM per device.

```python
import math
import jax
import jax.numpy as jnp
import numpy as np
from jax import lax

COLS = 1024
ROWS_DEV = 2048
S_DEV = 256
COL_DEV = 128
ROWS = 131072
SAMPLES = 16384
CAP = 8
N_ROW = 64
N_COL = 8


def draw_matrix(key, part):
    key = jax.random.fold_in(key, 11)
    key_column, key_rowscale, key_values = jax.random.split(key, 3)
    column_scale = jnp.exp(jax.random.uniform(key_column, (COLS,), jnp.float32, math.log(0.5), math.log(5.0)))
    row_scale = jnp.exp(jax.random.uniform(key_rowscale, (ROWS, 1), jnp.float32, math.log(0.3), math.log(3.0)))
    values = jnp.clip(jax.random.normal(key_values, (ROWS, COLS), jnp.float32), -6.0, 6.0)
    return (values * row_scale * column_scale[None, :]).astype(jnp.float32)


def draw_row_signs(key, part):
    key = jax.random.fold_in(key, 12)
    return 2 * jax.random.randint(key, (ROWS,), 0, 2, dtype=jnp.int32) - 1


def touch_ends(drawn, own_key, least, high):
    longest = drawn.shape.index(max(drawn.shape))
    spots = []
    for shift in (0, 1):
        where = [jax.random.randint(jax.random.fold_in(own_key, axis), (), 0, length) for axis, length in enumerate(drawn.shape)]
        where[longest] = (where[longest] + shift) % drawn.shape[longest]
        spots.append(tuple(where))
    return drawn.at[spots[0]].set(least).at[spots[1]].set(high)


def deal_out(rng, own, number, rows, number_of, top, reach, slope):
    sequence = jax.random.permutation(rng, number_of)
    crowded, ordinary = portions_of(number_of, rows * top, reach, slope, True), portions_of(number_of, rows * top, reach, slope, False)
    places = jnp.arange(number_of)

    def named(lengths, offset_by):
        used = int((lengths > 0).sum())
        fixed = max(1, used // 4)
        shifted = fixed + (places - fixed + offset_by * (used - fixed)) % max(1, number_of - fixed)
        return jnp.zeros((number_of,), jnp.int32).at[sequence[jnp.where(places < fixed, places, shifted)]].set(jnp.asarray(lengths, jnp.int32))

    lengths = jnp.where(number % 4 == 0, named(crowded, number // 4), named(ordinary, number - number // 4 - 1))
    mixed = jax.random.permutation(jax.random.fold_in(own, 3), number_of)
    source_of, sink = mixed[0:number_of // 2 * 2:2], mixed[1:number_of // 2 * 2:2]
    room = jnp.minimum(lengths[source_of] - 1, reach - lengths[sink]) // 2
    room = jnp.where((source_of == sequence[0]) | (sink == sequence[0]) | (lengths[sink] == 0), 0, jnp.maximum(room, 0))
    shifted = jax.random.randint(jax.random.fold_in(own, 4), (number_of // 2,), 0, 1 << 20) % (room + 1)
    lengths = lengths.at[source_of].add(-shifted).at[sink].add(shifted)
    labels = jnp.searchsorted(jnp.cumsum(lengths), jnp.arange(rows * top), side="right").astype(jnp.int32)
    listing = labels.reshape(top, rows).T
    listing = listing[jax.random.permutation(jax.random.fold_in(own, 1), rows)]
    offset_by = jax.random.randint(jax.random.fold_in(own, 2), (rows, 1), 0, top)
    return jnp.take_along_axis(listing, (jnp.arange(top)[None, :] + offset_by) % top, axis=1)


def portions_of(count, total, most, slope, full):
    loads = [(1 << 20) // math.isqrt(grade ** slope) + 1 for grade in range(1, count + 1)]
    largest = most if full else min(most, max(-(-total // count), total * loads[0] // sum(loads)))
    least = 1 if total - largest >= count - 1 else 0
    counts, spare = [largest] + [least] * (count - 1), total - largest - least * (count - 1)
    while spare > 0:
        free = [i for i in range(1, count) if counts[i] < largest] or [i for i in range(1, count) if counts[i] < most]
        whole, budget = sum([loads[i] for i in free]), spare
        for i in free:
            more = min(most - counts[i], max(1, budget * loads[i] // whole), spare)
            counts[i] = counts[i] + more
            spare = spare - more
    return np.array(counts)


def setup_inputs(seed: int = 0) -> dict:
    key_of = jax.random.split(jax.random.key(seed), 5)
    matrix = draw_matrix(jax.random.fold_in(key_of[4], 71), 0)
    row_signs = draw_row_signs(jax.random.fold_in(key_of[4], 71), 0)
    sample_block_keys = jax.random.split(jax.random.fold_in(key_of[2], 1), SAMPLES // S_DEV)
    sample_block_turns = jax.random.permutation(jax.random.fold_in(key_of[2], 3), SAMPLES // S_DEV)
    sample_block = jax.vmap(lambda own, number: deal_out(jax.random.fold_in(key_of[2], 2), own, number, S_DEV, N_ROW, 1, CAP, 2))(sample_block_keys, sample_block_turns).reshape((SAMPLES, 1))
    sample_offset = touch_ends(jax.random.randint(key_of[3], (SAMPLES,), 0, ROWS_DEV), jax.random.fold_in(key_of[3], 1), 0, ROWS_DEV - 1).astype(jnp.int32)
    return dict(matrix=matrix, row_signs=row_signs, sample_block=sample_block, sample_offset=sample_offset)


highest = lax.Precision.HIGHEST

def walsh_table(order):
    indices = jnp.arange(order, dtype=jnp.int32)
    parity = jnp.zeros((order, order), jnp.int32)
    for bitpos in range(max(order.bit_length() - 1, 0)):
        column = jnp.bitwise_and(jnp.right_shift(indices, bitpos), 1)
        parity = jnp.bitwise_xor(parity, column[:, None] * column[None, :])
    return (1 - 2 * parity).astype(jnp.float32)

def reference(matrix, row_signs, sample_block, sample_offset):
    total_rows = ROWS_DEV * N_ROW
    row_block = ROWS_DEV // N_ROW
    outer = ROWS_DEV // 64
    factor_norm = 1.0 / math.sqrt(total_rows)
    w_outer = walsh_table(outer)
    w_inner = walsh_table(64)
    w_cross = walsh_table(N_ROW)
    signed = matrix * row_signs.astype(jnp.float32)[:, None]
    blocks = sample_block[:, 0].astype(jnp.int32)
    wanted = sample_offset // row_block * ROWS_DEV + blocks * row_block + sample_offset % row_block
    wanted = wanted.astype(jnp.int32)

    def column_block(number):
        piece = lax.dynamic_slice_in_dim(signed, number * COL_DEV, COL_DEV, 1)
        piece = piece.reshape(N_ROW, outer, 64, COL_DEV)
        piece = jnp.einsum('ai,pijc->pajc', w_outer, piece, precision=highest)
        piece = jnp.einsum('bj,pajc->pabc', w_inner, piece, precision=highest)
        piece = jnp.einsum('qp,pabc->qabc', w_cross, piece, precision=highest) * factor_norm
        return jnp.take(piece.reshape(total_rows, COL_DEV), wanted, axis=0)
    pieces = lax.map(column_block, jnp.arange(N_COL, dtype=jnp.int32))
    sketch = jnp.transpose(pieces, (1, 0, 2)).reshape(SAMPLES, COLS)
    gram = jnp.dot(sketch.T.astype(jnp.float32), sketch.astype(jnp.float32), precision=highest, preferred_element_type=jnp.float32) / SAMPLES
    return (sketch, jnp.linalg.cholesky(gram))
```

```python
import functools
import math

import jax
import jax.numpy as jnp
from jax import lax
from jax.experimental import pallas as pl
from jax.experimental.pallas import tpu as pltpu
from jax.sharding import PartitionSpec as P

highest = lax.Precision.HIGHEST


def walsh_table(order):
    indices = jnp.arange(order, dtype=jnp.int32)
    parity = jnp.zeros((order, order), jnp.int32)
    for bitpos in range(max(order.bit_length() - 1, 0)):
        column = jnp.bitwise_and(jnp.right_shift(indices, bitpos), 1)
        parity = jnp.bitwise_xor(parity, column[:, None] * column[None, :])
    return (1 - 2 * parity).astype(jnp.float32)


f32, bf16 = jnp.float32, jnp.bfloat16
TN = (((0,), (0,)), ((), ()))
PAN = 128
BLK = 16


def panel_factor(aug, upan):
    cur = aug[0:BLK, :]
    nblk = PAN // BLK
    for t in range(nblk):
        lo = t * BLK
        last = t == nblk - 1
        x = cur[:, lo:lo + BLK]
        C = [jnp.broadcast_to(x[:, k:k + 1], (BLK, PAN)) for k in range(BLK)]
        R = [cur[:, 0:PAN], cur[:, PAN:2 * PAN]]
        if not last:
            xt = jnp.transpose(cur[:, 0:PAN])[lo + BLK:lo + 2 * BLK, :]
            N = [jnp.broadcast_to(xt[:, k:k + 1], (BLK, PAN)) for k in range(BLK)]
            nxt = aug[lo + BLK:lo + 2 * BLK, :]
            if t > 0:
                done = upan[0:lo, :]
                nxt = nxt - lax.dot_general(done[:, lo + BLK:lo + 2 * BLK], done, TN,
                                            precision=lax.Precision.HIGHEST, preferred_element_type=f32)
            Rn = [nxt[:, 0:PAN], nxt[:, PAN:2 * PAN]]
        for k in range(BLK):
            rs = lax.rsqrt(C[k][k:k + 1, :])
            u = [R[h][k:k + 1, :] * rs for h in range(2)]
            for h in range(2):
                upan[lo + k:lo + k + 1, h * PAN:(h + 1) * PAN] = u[h]
            L = C[k] * rs
            if not last:
                Nl = N[k] * rs
            for c in range(k + 1, BLK):
                m = L[c:c + 1, :]
                if c < 8:
                    C[c] = C[c] - L * m
                else:
                    C[c] = C[c] - L * m
                if not last:
                    N[c] = N[c] - Nl * m
            for h in range(2):
                if k < BLK - 1:
                    R[h] = R[h] - L * u[h]
                if not last:
                    Rn[h] = Rn[h] - Nl * u[h]
        if not last:
            cur = jnp.concatenate(Rn, axis=1)


def chol_kernel(n, g_ref, out_ref, s, u, aug, upan):
    np_ = n // PAN
    s[...] = g_ref[...]
    u[...] = jnp.zeros_like(u)
    ri = lax.broadcasted_iota(jnp.int32, (PAN, PAN), 0)
    ci = lax.broadcasted_iota(jnp.int32, (PAN, PAN), 1)

    def body(p, _):
        base = pl.multiple_of(p * PAN, PAN)
        aug[:, 0:PAN] = s[pl.ds(base, PAN), pl.ds(base, PAN)]
        aug[:, PAN:] = jnp.where(ri == ci, 1.0, 0.0).astype(f32)
        panel_factor(aug, upan)
        u[pl.ds(base, PAN), pl.ds(base, PAN)] = jnp.where(ri <= ci, upan[:, 0:PAN], 0.0)
        for pp in range(np_ - 1):
            @pl.when(p == pp)
            def _():
                a0, a1, rest = pp * PAN, (pp + 1) * PAN, n
                linv = jnp.where(ri >= ci, upan[:, PAN:], 0.0)
                w = lax.dot_general(linv, s[a0:a1, a1:], (((1,), (0,)), ((), ())),
                                    precision=lax.Precision.HIGHEST, preferred_element_type=f32)
                u[a0:a1, a1:] = w
                for q in range(pp + 1, np_):
                    q0 = q * PAN
                    s[q0:q0 + PAN, q0:] = s[q0:q0 + PAN, q0:] - lax.dot_general(
                        w[:, q0 - a1:q0 - a1 + PAN], w[:, q0 - a1:], TN,
                        precision=lax.Precision.HIGHEST, preferred_element_type=f32)
        return 0

    lax.fori_loop(0, np_, body, 0)
    out_ref[...] = u[...]


def chol(g):
    n = g.shape[0]
    return pl.pallas_call(
        functools.partial(chol_kernel, n),
        out_shape=jax.ShapeDtypeStruct((n, n), f32),
        in_specs=[pl.BlockSpec(memory_space=pltpu.VMEM)],
        out_specs=pl.BlockSpec(memory_space=pltpu.VMEM),
        scratch_shapes=[pltpu.VMEM((n, n), f32), pltpu.VMEM((n, n), f32),
                        pltpu.VMEM((PAN, 2 * PAN), f32), pltpu.VMEM((PAN, 2 * PAN), f32)],
        compiler_params=pltpu.CompilerParams(vmem_limit_bytes=48 * 2**20),
        name="chol",
    )(g)


def slot_numbers(blocks, devices):
    onehot = (blocks[:, None] == jnp.arange(devices, dtype=jnp.int32)[None, :]).astype(jnp.int32)
    before = jnp.cumsum(onehot, axis=0) - onehot
    return jnp.sum(before * onehot, axis=1)


def shards(matrix, row_signs, sample_block, sample_offset):
    local_rows, col_width = matrix.shape
    devices = lax.axis_size("row")
    row_block = local_rows // devices
    outer = local_rows // 64
    factor_norm = 1.0 / math.sqrt(devices * local_rows)
    signed = matrix * row_signs.astype(jnp.float32)[:, None]
    signed = signed.reshape(outer, 64, col_width)
    signed = jnp.einsum("ai,ijc->ajc", walsh_table(outer), signed, precision=highest)
    signed = jnp.einsum("bj,ajc->abc", walsh_table(64), signed, precision=highest)
    sectioned = signed.reshape(devices, row_block, col_width)
    w_cross = walsh_table(devices)
    mixed = (
        jnp.einsum(
            "qp,pic->qic",
            w_cross,
            lax.all_to_all(sectioned, "row", split_axis=0, concat_axis=0, tiled=True),
            precision=highest,
        )
        * factor_norm
    )
    holder_table = mixed.reshape(devices * row_block, col_width)
    own_count = sample_offset.shape[0]
    capacity = max(2, 2 * own_count // devices)
    blocks = sample_block[:, 0]
    slots = slot_numbers(blocks, devices)
    outgoing = jnp.zeros((devices, capacity), jnp.int32).at[blocks, slots].set(sample_offset)
    requests = lax.all_to_all(outgoing, "row", split_axis=0, concat_axis=0, tiled=True)
    answers = jnp.take(holder_table, requests.reshape(-1), axis=0).reshape(
        devices, capacity, col_width
    )
    returned = lax.all_to_all(answers, "row", split_axis=0, concat_axis=0, tiled=True)
    sketch = returned[blocks, slots]
    samples_total = own_count * devices
    panel = lax.all_gather(sketch, "col", axis=1, tiled=True)
    local_part = jnp.dot(panel.T, sketch, precision=highest, preferred_element_type=jnp.float32)
    pieces = local_part.reshape(devices, -1, col_width)
    pieces = lax.all_to_all(pieces, "row", split_axis=0, concat_axis=0, tiled=True)
    summed = jnp.sum(pieces, axis=0) / samples_total
    gram = lax.all_gather(lax.all_gather(summed, "col", axis=1, tiled=True), "row", axis=0, tiled=True)
    upper = chol(gram)
    own = lax.dynamic_slice_in_dim(upper, lax.axis_index("col") * col_width, col_width, 0)
    return sketch, own.T


def solution(mesh):
    placed = (P("row", "col"), P("row"), P("row", None), P("row"))
    return jax.shard_map(
        shards,
        mesh=mesh,
        in_specs=placed,
        out_specs=(P("row", "col"), P(None, "col")),
        check_vma=False,
    )
```

```python
import functools
import math

import jax
import jax.numpy as jnp
from jax import lax
from jax.experimental import pallas as pl
from jax.experimental.pallas import tpu as pltpu
from jax.sharding import PartitionSpec as P

f32, bf16 = jnp.float32, jnp.bfloat16
TN = (((0,), (0,)), ((), ()))
HI = lax.Precision.HIGHEST


def butterflies(v):
    n, step = len(v), 1
    while step < n:
        v = [v[i] + v[i + step] if not i & step else v[i - step] - v[i] for i in range(n)]
        step *= 2
    return v


def mix_pass(src, dst, rows, low, bits, scale=None):
    n, stride = 1 << bits, 1 << low
    tiles = stride // 8
    groups = rows // (n * stride)

    def body(t, _):
        g, j = t // tiles, t % tiles
        base = g * (n * stride) + j * 8
        v = [src[pl.ds(pl.multiple_of(base + i * stride, 8), 8), :] for i in range(n)]
        v = butterflies(v)
        for i in range(n):
            dst[pl.ds(pl.multiple_of(base + i * stride, 8), 8), :] = v[i] if scale is None else v[i] * scale
        return 0

    lax.fori_loop(0, groups * tiles, body, 0, unroll=2 if groups * tiles % 2 == 0 else 1)


def exchange_kernel(X, Z, C, norm, samples,
                    a_ref, sign_ref, blk_ref, off_ref,
                    gram_ref, sk_ref,
                    v, recv, table, req, reqr, reqs, own, owns, ans, ret, xall, part, xr, zs, zr, xg,
                    s_req, r_req, s_sec, r_sec, s_ans, r_ans, s_col, r_col, s_x, r_x, s_z, r_z,
                    s_zg, r_zg, s_xg, r_xg, s_cg, r_cg, l_sem):
    D = X * Z
    rows = a_ref.shape[0]
    rb = rows // D
    W = a_ref.shape[1]
    cap = ans.shape[0] // D
    S = blk_ref.shape[0]
    me, col = lax.axis_index("row"), lax.axis_index("col")
    mx, mz = me // Z, me % Z
    sib = col + 1 - 2 * (col % 2)

    def rcopy(src, dst, ss, rs, row=None, c=None):
        dev = {"row": row} if c is None else {"col": c}
        return pltpu.make_async_remote_copy(src_ref=src, dst_ref=dst, send_sem=ss, recv_sem=rs,
                                            device_id=dev, device_id_type=pl.DeviceIdType.MESH)

    bar = pltpu.get_barrier_semaphore()

    def greet(k, _):
        pl.semaphore_signal(bar, inc=1, device_id={"row": lax.rem(me + k, D)}, device_id_type=pl.DeviceIdType.MESH)
        return 0
    lax.fori_loop(1, D, greet, 0)
    ypeers = [lax.rem(col + 2 * k, C) for k in range(1, C // 2)]
    for c in [sib] + ypeers:
        pl.semaphore_signal(bar, inc=1, device_id={"col": c}, device_id_type=pl.DeviceIdType.MESH)

    blocks = blk_ref[...]
    lane = lax.broadcasted_iota(jnp.int32, (S, 128), 1)
    onehot = (blocks == lane).astype(f32)
    ri = lax.broadcasted_iota(jnp.int32, (S, S), 0)
    ci = lax.broadcasted_iota(jnp.int32, (S, S), 1)
    before = jnp.dot((ci < ri).astype(bf16), onehot.astype(bf16), preferred_element_type=f32)
    slot = jnp.sum(before * onehot, axis=1, keepdims=True)
    offs = jnp.transpose(jnp.concatenate(
        [off_ref[...].astype(f32), jnp.zeros((128 - S // 128, 128), f32)], axis=0))
    offc = jnp.concatenate([offs[:, k:k + 1] for k in range(S // 128)], axis=0)
    val = jnp.where(lane.astype(f32) == slot, offc - float(rows), 0.0)
    wanted = lax.dot_general(onehot, val, TN, precision=HI, preferred_element_type=f32) + float(rows)
    wanted = wanted.astype(jnp.int32)
    for j in range(D):
        req[j] = wanted[j:j + 1, :]
    place = (blocks.astype(f32) * float(cap) + slot)
    for k in range(S // 128):
        t = jnp.transpose(jnp.broadcast_to(place[k * 128:(k + 1) * 128, :], (128, 128)))
        own[k] = t[0:1, :].astype(jnp.int32)
    oc = pltpu.make_async_copy(own, owns, l_sem.at[0])
    oc.start()

    nb = rows // 128
    st = jnp.transpose(jnp.concatenate([sign_ref[...].astype(f32), jnp.zeros((128 - nb, 128), f32)], axis=0))
    for j in range(nb):
        v[j * 128:(j + 1) * 128, :] = a_ref[j * 128:(j + 1) * 128, :] * jnp.broadcast_to(st[:, j:j + 1], (128, W))

    def low_bits(g, _):
        base = pl.multiple_of(g * 64, 64)
        w = butterflies([v[pl.ds(base + k, 8, stride=8), :] for k in range(8)])
        for k in range(8):
            v[pl.ds(base + k, 8, stride=8), :] = w[k]
        return 0
    lax.fori_loop(0, rows // 64, low_bits, 0, unroll=2)
    left, low = rows.bit_length() - 1 - 3, 3
    while left:
        b = min(3, left)
        mix_pass(v, v, rows, low, b)
        low, left = low + b, left - b

    pl.semaphore_wait(bar, D - 1 + 1 + len(ypeers))

    def peer_of(k):
        return lax.rem(me + jnp.where(k % 2 == 1, (k + 1) // 2, D - k // 2), D)

    def sends(fn):
        def go(k, _):
            fn(peer_of(k)).start()
            return 0
        lax.fori_loop(1, D, go, 0)

    def waits(fn, recv_side):
        def go(k, _):
            c = fn(lax.rem(me + k, D))
            if recv_side:
                c.wait_recv()
            else:
                c.wait_send()
            return 0
        lax.fori_loop(1, D, go, 0)

    c_req = lambda j: rcopy(req.at[j], reqr.at[me], s_req.at[j], r_req.at[me], row=j)
    w_req = lambda j: rcopy(req.at[j], reqr.at[j], s_req.at[j], r_req.at[j], row=j)
    sec = lambda j: v.at[pl.ds(pl.multiple_of(j * rb, rb), rb), :]
    got = lambda j: recv.at[pl.ds(pl.multiple_of(j * rb, rb), rb), :]
    c_sec = lambda j: rcopy(sec(j), got(me), s_sec.at[j], r_sec.at[me], row=j)
    w_sec = lambda j: rcopy(sec(j), got(j), s_sec.at[j], r_sec.at[j], row=j)
    sends(c_req)
    sends(c_sec)
    reqr[me] = req[me]
    recv[pl.ds(pl.multiple_of(me * rb, rb), rb), :] = v[pl.ds(pl.multiple_of(me * rb, rb), rb), :]
    table[rows:rows + 8, :] = jnp.zeros((8, W), f32)
    waits(w_req, True)
    rc = pltpu.make_async_copy(reqr, reqs, l_sem.at[1])
    rc.start()
    rc.wait()
    oc.wait()
    waits(w_sec, True)

    lowb = rb.bit_length() - 1
    left, low, first = D.bit_length() - 1, lowb, True
    while left:
        b = min(3, left)
        left -= b
        mix_pass(recv if first else table, table, rows, low, b, norm if left == 0 else None)
        low, first = low + b, False

    def answer(j, _):
        for c in range(cap):
            ans[pl.ds(j * cap + c, 1), :] = table[pl.ds(jnp.clip(reqs[j, 0, c], 0, rows), 1), :]
        return 0
    lax.fori_loop(0, D, answer, 0, unroll=2)

    R = D * cap
    xall[col] = ans[...]
    c_col = lambda s, to: rcopy(xall.at[s], xall.at[s], s_col.at[s, 0 if to is None else 1 + to], r_col.at[s],
                                c=sib if to is None else ypeers[to])
    started = [c_col(col, None)] + [c_col(col, k) for k in range(len(ypeers))]
    for c in started[1:]:
        c.start()
    started[0].start()
    slots = lambda ref, j: ref.at[pl.ds(pl.multiple_of(j * cap, 8), cap), :]
    c_ans = lambda j: rcopy(slots(ans, j), slots(ret, me), s_ans.at[j], r_ans.at[me], row=j)
    w_ans = lambda j: rcopy(slots(ans, j), slots(ret, j), s_ans.at[j], r_ans.at[j], row=j)
    sends(c_ans)
    here = pl.ds(pl.multiple_of(me * cap, 8), cap)
    ret[here, :] = ans[here, :]

    mine = xall[col]

    def block(s):
        part[pl.ds(pl.multiple_of(s * W, W), W), :] = lax.dot_general(
            mine, xall[s], TN, precision=HI, preferred_element_type=f32)
    block(col)
    for k in (0, 2, 1) if len(ypeers) == 3 else range(len(ypeers)):
        s = ypeers[k]
        c_col(s, None).wait_recv()
        f = c_col(s, None)
        f.start()
        started.append(f)
        block(s)
    for k in range(C // 2):
        s = lax.rem(sib + 2 * k, C)
        c_col(s, None).wait_recv()
        block(s)

    q = C * W // X
    xs = lambda j: part.at[pl.ds(pl.multiple_of(j * q, q), q), :]
    c_x = lambda j: rcopy(xs(j), xr.at[mx], s_x.at[j], r_x.at[mx], row=j * Z + mz)
    w_x = lambda j: rcopy(xs(j), xr.at[j], s_x.at[j], r_x.at[j], row=j * Z + mz)
    xpeers = [lax.rem(mx + k, X) for k in range(1, X)]
    for j in xpeers:
        c_x(j).start()
    xr[mx] = part[pl.ds(pl.multiple_of(mx * q, q), q), :]

    waits(w_ans, True)

    def keep(t, _):
        k, base = t // 16, t % 16
        for e in range(8):
            i = jnp.clip(owns[k, 0, base * 8 + e], 0, R - 1)
            sk_ref[pl.ds(t * 8 + e, 1), :] = ret[pl.ds(i, 1), :]
        return 0
    lax.fori_loop(0, S // 8, keep, 0)

    for j in xpeers:
        w_x(j).wait_recv()
    acc = xr[0]
    for j in range(1, X):
        acc = acc + xr[j]
    e = q // Z
    zs[...] = acc.reshape(Z, e, W)
    zpeers = lambda k: lax.rem(mz + k, Z)
    c_z = lambda j: rcopy(zs.at[j], zr.at[mz], s_z.at[j], r_z.at[mz], row=mx * Z + j)
    w_z = lambda j: rcopy(zs.at[j], zr.at[j], s_z.at[j], r_z.at[j], row=mx * Z + j)
    for k in range(1, Z):
        c_z(zpeers(k)).start()
    zr[mz] = zs[mz]
    for k in range(1, Z):
        w_z(zpeers(k)).wait_recv()
    acc = zr[0]
    for j in range(1, Z):
        acc = acc + zr[j]
    xg[mx, pl.ds(pl.multiple_of(mz * e, e), e), :] = acc / samples
    ze = lambda x, j: xg.at[x, pl.ds(pl.multiple_of(j * e, e), e), :]
    c_zg = lambda j: rcopy(ze(mx, mz), ze(mx, mz), s_zg.at[j], r_zg.at[mz], row=mx * Z + j)
    w_zg = lambda j: rcopy(ze(mx, j), ze(mx, j), s_zg.at[j], r_zg.at[j], row=mx * Z + j)
    for k in range(1, Z):
        c_zg(zpeers(k)).start()
    for k in range(1, Z):
        w_zg(zpeers(k)).wait_recv()
    c_xg = lambda j: rcopy(xg.at[mx], xg.at[mx], s_xg.at[j], r_xg.at[mx], row=j * Z + mz)
    w_xg = lambda j: rcopy(xg.at[j], xg.at[j], s_xg.at[j], r_xg.at[j], row=j * Z + mz)
    for j in xpeers:
        c_xg(j).start()
    for j in xpeers:
        w_xg(j).wait_recv()
    gram_ref[col] = xg[...].reshape(C * W, W)
    c_cg = lambda s, to: rcopy(gram_ref.at[s], gram_ref.at[s], s_cg.at[s, 0 if to is None else 1 + to], r_cg.at[s],
                               c=sib if to is None else ypeers[to])
    out = [c_cg(col, None)] + [c_cg(col, k) for k in range(len(ypeers))]
    for c in out[1:]:
        c.start()
    out[0].start()
    for k in (0, 2, 1) if len(ypeers) == 3 else range(len(ypeers)):
        s = ypeers[k]
        c_cg(s, None).wait_recv()
        f = c_cg(s, None)
        f.start()
        out.append(f)
    for k in range(C // 2):
        c_cg(lax.rem(sib + 2 * k, C), None).wait_recv()

    waits(w_req, False)
    waits(w_sec, False)
    waits(w_ans, False)
    for c in started + out:
        c.wait_send()
    for j in xpeers:
        w_x(j).wait_send()
        w_xg(j).wait_send()
    for k in range(1, Z):
        w_z(zpeers(k)).wait_send()
        w_zg(zpeers(k)).wait_send()


def exchange(a, signs, blocks, offs, X, Z, C):
    rows, W = a.shape
    D = X * Z
    S = offs.shape[0]
    cap = max(2, 2 * S // D)
    rb = rows // D
    R = D * cap
    q = C * W // X
    V = pltpu.VMEM
    dma = pltpu.SemaphoreType.DMA
    return pl.pallas_call(
        functools.partial(exchange_kernel, X, Z, C, 1.0 / math.sqrt(D * rows), float(D * S)),
        out_shape=(jax.ShapeDtypeStruct((C, C * W, W), f32), jax.ShapeDtypeStruct((S, W), f32)),
        in_specs=[pl.BlockSpec(memory_space=V)] * 4,
        out_specs=(pl.BlockSpec(memory_space=V), pl.BlockSpec(memory_space=V)),
        scratch_shapes=[
            V((rows, W), f32), V((rows, W), f32), V((rows + 8, W), f32),
            V((D, 1, 128), jnp.int32), V((D, 1, 128), jnp.int32), pltpu.SMEM((D, 1, 128), jnp.int32),
            V((S // 128, 1, 128), jnp.int32), pltpu.SMEM((S // 128, 1, 128), jnp.int32),
            V((R, W), f32), V((R, W), f32), V((C, R, W), f32),
            V((C * W, W), f32), V((X, q, W), f32), V((Z, q // Z, W), f32), V((Z, q // Z, W), f32), V((X, q, W), f32),
            dma((D,)), dma((D,)), dma((D,)), dma((D,)), dma((D,)), dma((D,)),
            dma((C, 1 + C // 2)), dma((C,)), dma((X,)), dma((X,)), dma((Z,)), dma((Z,)),
            dma((Z,)), dma((Z,)), dma((X,)), dma((X,)), dma((C, 1 + C // 2)), dma((C,)), dma((2,)),
        ],
        compiler_params=pltpu.CompilerParams(collective_id=0, has_side_effects=True, vmem_limit_bytes=48 * 2**20),
        name="exchange",
    )(a, signs.reshape(rows // 128, 128), blocks, offs.reshape(S // 128, 128))


PAN = 128
BLK = 16


def panel_factor(aug, upan):
    cur = aug[0:BLK, :]
    nblk = PAN // BLK
    for t in range(nblk):
        lo = t * BLK
        last = t == nblk - 1
        x = cur[:, lo:lo + BLK]
        C = [jnp.broadcast_to(x[:, k:k + 1], (BLK, PAN)) for k in range(BLK)]
        R = [cur[:, 0:PAN], cur[:, PAN:2 * PAN]]
        if not last:
            xt = jnp.transpose(cur[:, 0:PAN])[lo + BLK:lo + 2 * BLK, :]
            N = [jnp.broadcast_to(xt[:, k:k + 1], (BLK, PAN)) for k in range(BLK)]
            nxt = aug[lo + BLK:lo + 2 * BLK, :]
            if t > 0:
                done = upan[0:lo, :]
                nxt = nxt - lax.dot_general(done[:, lo + BLK:lo + 2 * BLK], done, TN,
                                            precision=lax.Precision.HIGHEST, preferred_element_type=f32)
            Rn = [nxt[:, 0:PAN], nxt[:, PAN:2 * PAN]]
        for k in range(BLK):
            rs = lax.rsqrt(C[k][k:k + 1, :])
            u = [R[h][k:k + 1, :] * rs for h in range(2)]
            for h in range(2):
                upan[lo + k:lo + k + 1, h * PAN:(h + 1) * PAN] = u[h]
            L = C[k] * rs
            if not last:
                Nl = N[k] * rs
            for c in range(k + 1, BLK):
                m = L[c:c + 1, :]
                if c < 8:
                    C[c] = C[c] - L * m
                else:
                    C[c] = C[c] - L * m
                if not last:
                    N[c] = N[c] - Nl * m
            for h in range(2):
                if k < BLK - 1:
                    R[h] = R[h] - L * u[h]
                if not last:
                    Rn[h] = Rn[h] - Nl * u[h]
        if not last:
            cur = jnp.concatenate(Rn, axis=1)


def chol_kernel(n, col_name, g_ref, out_ref, s, u, aug, upan):
    np_ = n // PAN
    for i in range(np_):
        for j in range(np_):
            s[i * PAN:(i + 1) * PAN, j * PAN:(j + 1) * PAN] = g_ref[i, j * PAN:(j + 1) * PAN, :]
    u[...] = jnp.zeros_like(u)
    ri = lax.broadcasted_iota(jnp.int32, (PAN, PAN), 0)
    ci = lax.broadcasted_iota(jnp.int32, (PAN, PAN), 1)

    def body(p, _):
        base = pl.multiple_of(p * PAN, PAN)
        aug[:, 0:PAN] = s[pl.ds(base, PAN), pl.ds(base, PAN)]
        aug[:, PAN:] = jnp.where(ri == ci, 1.0, 0.0).astype(f32)
        panel_factor(aug, upan)
        u[pl.ds(base, PAN), pl.ds(base, PAN)] = jnp.where(ri <= ci, upan[:, 0:PAN], 0.0)
        for pp in range(np_ - 1):
            @pl.when(p == pp)
            def _():
                a0, a1, rest = pp * PAN, (pp + 1) * PAN, n
                linv = jnp.where(ri >= ci, upan[:, PAN:], 0.0)
                w = lax.dot_general(linv, s[a0:a1, a1:], (((1,), (0,)), ((), ())),
                                    precision=lax.Precision.HIGHEST, preferred_element_type=f32)
                u[a0:a1, a1:] = w
                for q in range(pp + 1, np_):
                    q0 = q * PAN
                    s[q0:q0 + PAN, q0:] = s[q0:q0 + PAN, q0:] - lax.dot_general(
                        w[:, q0 - a1:q0 - a1 + PAN], w[:, q0 - a1:], TN,
                        precision=lax.Precision.HIGHEST, preferred_element_type=f32)
        return 0

    lax.fori_loop(0, np_, body, 0)
    mine = pl.multiple_of(lax.axis_index(col_name) * PAN, PAN)
    for j in range(np_):
        out_ref[j * PAN:(j + 1) * PAN, :] = jnp.transpose(u[pl.ds(mine, PAN), j * PAN:(j + 1) * PAN])


def chol(g):
    n = g.shape[1]
    return pl.pallas_call(
        functools.partial(chol_kernel, n, "col"),
        out_shape=jax.ShapeDtypeStruct((n, PAN), f32),
        in_specs=[pl.BlockSpec(memory_space=pltpu.VMEM)],
        out_specs=pl.BlockSpec(memory_space=pltpu.VMEM),
        scratch_shapes=[pltpu.VMEM((n, n), f32), pltpu.VMEM((n, n), f32),
                        pltpu.VMEM((PAN, 2 * PAN), f32), pltpu.VMEM((PAN, 2 * PAN), f32)],
        compiler_params=pltpu.CompilerParams(vmem_limit_bytes=48 * 2**20),
        name="chol",
    )(g)


def solution(mesh):
    x_size, z_size, c_size = 4, mesh.shape["row"] // 4, mesh.shape["col"]

    def shards(matrix, row_signs, sample_block, sample_offset):
        gram, sketch = exchange(matrix, row_signs, sample_block, sample_offset, x_size, z_size, c_size)
        return sketch, chol(gram)

    placed = (P("row", "col"), P("row"), P("row", None), P("row"))
    return jax.shard_map(
        shards,
        mesh=mesh,
        in_specs=placed,
        out_specs=(P("row", "col"), P(None, "col")),
        check_vma=False,
    )
```

```python
import functools
import math

import jax
import jax.numpy as jnp
from jax import lax
from jax.experimental import pallas as pl
from jax.experimental.pallas import tpu as pltpu
from jax.sharding import PartitionSpec as P

f32, bf16 = jnp.float32, jnp.bfloat16
TN = (((0,), (0,)), ((), ()))
HI = lax.Precision.HIGHEST


def butterflies(v):
    n, step = len(v), 1
    while step < n:
        v = [v[i] + v[i + step] if not i & step else v[i - step] - v[i] for i in range(n)]
        step *= 2
    return v


def mix_pass(src, dst, rows, low, bits, scale=None):
    n, stride = 1 << bits, 1 << low
    tiles = stride // 8
    groups = rows // (n * stride)

    def body(t, _):
        g, j = t // tiles, t % tiles
        base = g * (n * stride) + j * 8
        v = [src[pl.ds(pl.multiple_of(base + i * stride, 8), 8), :] for i in range(n)]
        v = butterflies(v)
        for i in range(n):
            dst[pl.ds(pl.multiple_of(base + i * stride, 8), 8), :] = v[i] if scale is None else v[i] * scale
        return 0

    lax.fori_loop(0, groups * tiles, body, 0, unroll=2 if groups * tiles % 2 == 0 else 1)


PAN = 128
BLK = 16


def panel_factor(aug, upan):
    cur = aug[0:BLK, :]
    nblk = PAN // BLK
    for t in range(nblk):
        lo = t * BLK
        last = t == nblk - 1
        x = cur[:, lo:lo + BLK]
        C = [jnp.broadcast_to(x[:, k:k + 1], (BLK, PAN)) for k in range(BLK)]
        R = [cur[:, 0:PAN], cur[:, PAN:2 * PAN]]
        if not last:
            xt = jnp.transpose(cur[:, 0:PAN])[lo + BLK:lo + 2 * BLK, :]
            N = [jnp.broadcast_to(xt[:, k:k + 1], (BLK, PAN)) for k in range(BLK)]
            nxt = aug[lo + BLK:lo + 2 * BLK, :]
            if t > 0:
                done = upan[0:lo, :]
                nxt = nxt - lax.dot_general(done[:, lo + BLK:lo + 2 * BLK], done, TN,
                                            precision=lax.Precision.HIGHEST, preferred_element_type=f32)
            Rn = [nxt[:, 0:PAN], nxt[:, PAN:2 * PAN]]
        for k in range(BLK):
            rs = lax.rsqrt(C[k][k:k + 1, :])
            u = [R[h][k:k + 1, :] * rs for h in range(2)]
            for h in range(2):
                upan[lo + k:lo + k + 1, h * PAN:(h + 1) * PAN] = u[h]
            L = C[k] * rs
            if not last:
                Nl = N[k] * rs
            for c in range(k + 1, BLK):
                m = L[c:c + 1, :]
                if c < 8:
                    C[c] = C[c] - L * m
                else:
                    C[c] = C[c] - L * m
                if not last:
                    N[c] = N[c] - Nl * m
            for h in range(2):
                if k < BLK - 1:
                    R[h] = R[h] - L * u[h]
                if not last:
                    Rn[h] = Rn[h] - Nl * u[h]
        if not last:
            cur = jnp.concatenate(Rn, axis=1)


def exchange_kernel(X, Z, C, norm, samples,
                    a_ref, sign_ref, blk_ref, off_ref,
                    fac_ref, sk_ref,
                    v, recv, table, req, reqr, reqs, own, owns, ans, ret, xall, part, xr, zs, zr, gb, u, aug, upan,
                    s_req, r_req, s_sec, r_sec, s_ans, r_ans, s_col, r_col, s_x, r_x, s_z, r_z,
                    s_zg, r_zg, s_xg, r_xg, s_cg, s_fw, r_cg, l_sem):
    D = X * Z
    rows = a_ref.shape[0]
    rb = rows // D
    W = a_ref.shape[1]
    cap = ans.shape[0] // D
    S = blk_ref.shape[0]
    me, col = lax.axis_index("row"), lax.axis_index("col")
    mx, mz = me // Z, me % Z
    sib = col + 1 - 2 * (col % 2)

    def rcopy(src, dst, ss, rs, row=None, c=None):
        dev = {"row": row} if c is None else {"col": c}
        return pltpu.make_async_remote_copy(src_ref=src, dst_ref=dst, send_sem=ss, recv_sem=rs,
                                            device_id=dev, device_id_type=pl.DeviceIdType.MESH)

    bar = pltpu.get_barrier_semaphore()

    def greet(k, _):
        pl.semaphore_signal(bar, inc=1, device_id={"row": lax.rem(me + k, D)}, device_id_type=pl.DeviceIdType.MESH)
        return 0
    lax.fori_loop(1, D, greet, 0)
    ypeers = [lax.rem(col + 2 * k, C) for k in range(1, C // 2)]
    for c in [sib] + ypeers:
        pl.semaphore_signal(bar, inc=1, device_id={"col": c}, device_id_type=pl.DeviceIdType.MESH)

    blocks = blk_ref[...]
    lane = lax.broadcasted_iota(jnp.int32, (S, 128), 1)
    onehot = (blocks == lane).astype(f32)
    ri = lax.broadcasted_iota(jnp.int32, (S, S), 0)
    ci = lax.broadcasted_iota(jnp.int32, (S, S), 1)
    before = jnp.dot((ci < ri).astype(bf16), onehot.astype(bf16), preferred_element_type=f32)
    slot = jnp.sum(before * onehot, axis=1, keepdims=True)
    offs = jnp.transpose(jnp.concatenate(
        [off_ref[...].astype(f32), jnp.zeros((128 - S // 128, 128), f32)], axis=0))
    offc = jnp.concatenate([offs[:, k:k + 1] for k in range(S // 128)], axis=0)
    val = jnp.where(lane.astype(f32) == slot, offc - float(rows), 0.0)
    wanted = lax.dot_general(onehot, val, TN, precision=HI, preferred_element_type=f32) + float(rows)
    wanted = wanted.astype(jnp.int32)
    for j in range(D):
        req[j] = wanted[j:j + 1, :]
    place = (blocks.astype(f32) * float(cap) + slot)
    for k in range(S // 128):
        t = jnp.transpose(jnp.broadcast_to(place[k * 128:(k + 1) * 128, :], (128, 128)))
        own[k] = t[0:1, :].astype(jnp.int32)
    oc = pltpu.make_async_copy(own, owns, l_sem.at[0])
    oc.start()

    nb = rows // 128
    st = jnp.transpose(jnp.concatenate([sign_ref[...].astype(f32), jnp.zeros((128 - nb, 128), f32)], axis=0))
    for j in range(nb):
        v[j * 128:(j + 1) * 128, :] = a_ref[j * 128:(j + 1) * 128, :] * jnp.broadcast_to(st[:, j:j + 1], (128, W))

    def low_bits(g, _):
        base = pl.multiple_of(g * 64, 64)
        w = butterflies([v[pl.ds(base + k, 8, stride=8), :] for k in range(8)])
        for k in range(8):
            v[pl.ds(base + k, 8, stride=8), :] = w[k]
        return 0
    lax.fori_loop(0, rows // 64, low_bits, 0, unroll=2)
    left, low = rows.bit_length() - 1 - 3, 3
    while left:
        b = min(3, left)
        mix_pass(v, v, rows, low, b)
        low, left = low + b, left - b

    pl.semaphore_wait(bar, D - 1 + 1 + len(ypeers))

    def peer_of(k):
        return lax.rem(me + jnp.where(k % 2 == 1, (k + 1) // 2, D - k // 2), D)

    def sends(fn):
        def go(k, _):
            fn(peer_of(k)).start()
            return 0
        lax.fori_loop(1, D, go, 0)

    def waits(fn, recv_side):
        def go(k, _):
            c = fn(lax.rem(me + k, D))
            if recv_side:
                c.wait_recv()
            else:
                c.wait_send()
            return 0
        lax.fori_loop(1, D, go, 0)

    c_req = lambda j: rcopy(req.at[j], reqr.at[me], s_req.at[j], r_req.at[me], row=j)
    w_req = lambda j: rcopy(req.at[j], reqr.at[j], s_req.at[j], r_req.at[j], row=j)
    sec = lambda j: v.at[pl.ds(pl.multiple_of(j * rb, rb), rb), :]
    got = lambda j: recv.at[pl.ds(pl.multiple_of(j * rb, rb), rb), :]
    c_sec = lambda j: rcopy(sec(j), got(me), s_sec.at[j], r_sec.at[me], row=j)
    w_sec = lambda j: rcopy(sec(j), got(j), s_sec.at[j], r_sec.at[j], row=j)
    sends(c_req)
    sends(c_sec)
    reqr[me] = req[me]
    recv[pl.ds(pl.multiple_of(me * rb, rb), rb), :] = v[pl.ds(pl.multiple_of(me * rb, rb), rb), :]
    table[rows:rows + 8, :] = jnp.zeros((8, W), f32)
    waits(w_req, True)
    rc = pltpu.make_async_copy(reqr, reqs, l_sem.at[1])
    rc.start()
    rc.wait()
    oc.wait()
    waits(w_sec, True)

    lowb = rb.bit_length() - 1
    left, low, first = D.bit_length() - 1, lowb, True
    while left:
        b = min(3, left)
        left -= b
        mix_pass(recv if first else table, table, rows, low, b, norm if left == 0 else None)
        low, first = low + b, False

    def answer(j, _):
        for c in range(cap):
            ans[pl.ds(j * cap + c, 1), :] = table[pl.ds(jnp.clip(reqs[j, 0, c], 0, rows), 1), :]
        return 0
    lax.fori_loop(0, D, answer, 0, unroll=2)

    R = D * cap
    xall[col] = ans[...]
    c_col = lambda s, to: rcopy(xall.at[s], xall.at[s], s_col.at[s, 0 if to is None else 1 + to], r_col.at[s],
                                c=sib if to is None else ypeers[to])
    started = [c_col(col, None)] + [c_col(col, k) for k in range(len(ypeers))]
    for c in started[1:]:
        c.start()
    started[0].start()
    slots = lambda ref, j: ref.at[pl.ds(pl.multiple_of(j * cap, 8), cap), :]
    c_ans = lambda j: rcopy(slots(ans, j), slots(ret, me), s_ans.at[j], r_ans.at[me], row=j)
    w_ans = lambda j: rcopy(slots(ans, j), slots(ret, j), s_ans.at[j], r_ans.at[j], row=j)
    sends(c_ans)
    here = pl.ds(pl.multiple_of(me * cap, 8), cap)
    ret[here, :] = ans[here, :]

    mine = jnp.transpose(xall[col])

    def block(s):
        part[pl.ds(pl.multiple_of(s * W, W), W), :] = jnp.transpose(
            jnp.dot(mine, xall[s], precision=HI, preferred_element_type=f32))
    block(col)
    for k in (0, 2, 1) if len(ypeers) == 3 else range(len(ypeers)):
        s = ypeers[k]
        c_col(s, None).wait_recv()
        f = c_col(s, None)
        f.start()
        started.append(f)
        block(s)
    for k in range(C // 2):
        s = lax.rem(sib + 2 * k, C)
        c_col(s, None).wait_recv()
        block(s)

    q = C * W // X
    xs = lambda j: part.at[pl.ds(pl.multiple_of(j * q, q), q), :]
    c_x = lambda j: rcopy(xs(j), xr.at[mx], s_x.at[j], r_x.at[mx], row=j * Z + mz)
    w_x = lambda j: rcopy(xs(j), xr.at[j], s_x.at[j], r_x.at[j], row=j * Z + mz)
    xpeers = [lax.rem(mx + k, X) for k in range(1, X)]
    for j in xpeers:
        c_x(j).start()
    xr[mx] = part[pl.ds(pl.multiple_of(mx * q, q), q), :]

    waits(w_ans, True)

    def keep(t, _):
        k, base = t // 16, t % 16
        for e in range(8):
            i = jnp.clip(owns[k, 0, base * 8 + e], 0, R - 1)
            sk_ref[pl.ds(t * 8 + e, 1), :] = ret[pl.ds(i, 1), :]
        return 0
    lax.fori_loop(0, S // 8, keep, 0)

    for j in xpeers:
        w_x(j).wait_recv()
    acc = xr[0]
    for j in range(1, X):
        acc = acc + xr[j]
    e = q // Z
    zs[...] = acc.reshape(Z, e, W)
    zpeers = lambda k: lax.rem(mz + k, Z)
    c_z = lambda j: rcopy(zs.at[j], zr.at[mz], s_z.at[j], r_z.at[mz], row=mx * Z + j)
    w_z = lambda j: rcopy(zs.at[j], zr.at[j], s_z.at[j], r_z.at[j], row=mx * Z + j)
    for k in range(1, Z):
        c_z(zpeers(k)).start()
    zr[mz] = zs[mz]
    for k in range(1, Z):
        w_z(zpeers(k)).wait_recv()
    acc = zr[0]
    for j in range(1, Z):
        acc = acc + zr[j]
    gb[col, pl.ds(pl.multiple_of(mx * q + mz * e, e), e), :] = acc / samples
    ze = lambda j: gb.at[col, pl.ds(pl.multiple_of(mx * q + j * e, e), e), :]
    c_zg = lambda j: rcopy(ze(mz), ze(mz), s_zg.at[j], r_zg.at[mz], row=mx * Z + j)
    w_zg = lambda j: rcopy(ze(j), ze(j), s_zg.at[j], r_zg.at[j], row=mx * Z + j)
    for k in range(1, Z):
        c_zg(zpeers(k)).start()
    for k in range(1, Z):
        w_zg(zpeers(k)).wait_recv()
    per = C // X
    gblk = lambda s, p: gb.at[s, pl.ds(pl.multiple_of(p * W, W), W), :]
    c_xg = lambda p, j: rcopy(gblk(col, p), gblk(col, p), s_xg.at[p, j], r_xg.at[p], row=j * Z + mz)
    c_cg = lambda p, k: rcopy(gblk(col, p), gblk(col, p), s_cg.at[p, k], r_cg.at[col, p], c=ypeers[k])
    c_fw = lambda s, p: rcopy(gblk(s, p), gblk(s, p), s_fw.at[s, p], r_cg.at[s, p], c=sib)

    def along_x(p):
        @pl.when((mx == p // per) & (p <= col))
        def _():
            for j in xpeers:
                c_xg(p, j).start()

    def over_col(p):
        @pl.when(p <= col)
        def _():
            @pl.when(mx != p // per)
            def _():
                c_xg(p, mx).wait_recv()
            for k in (1, 0, 2) if len(ypeers) == 3 else range(len(ypeers)):
                c_cg(p, k).start()
            c_fw(col, p).start()

    def pass_on(p):
        for s in ypeers:
            @pl.when(p <= s)
            def _():
                c_fw(s, p).wait_recv()
                c_fw(s, p).start()

    def arrived(p):
        for k in range(C // 2):
            s = lax.rem(sib + 2 * k, C)

            @pl.when(p <= s)
            def _():
                c_fw(s, p).wait_recv()

    def each(fn, lo, hi):
        lax.fori_loop(lo, hi, lambda p, _: (fn(p), 0)[1], 0)
    each(along_x, 0, C)
    each(over_col, 0, 2)
    pass_on(0)

    u[...] = jnp.zeros_like(u)
    pr = lax.broadcasted_iota(jnp.int32, (W, W), 0)
    pc = lax.broadcasted_iota(jnp.int32, (W, W), 1)

    def panel(p, _):
        @pl.when(p + 2 < C)
        def _():
            over_col(p + 2)

        @pl.when(p + 1 < C)
        def _():
            pass_on(p + 1)
        arrived(p)
        base = pl.multiple_of(p * W, W)
        for pp in range(C):
            @pl.when(p == pp)
            def _():
                a0 = pp * W
                for t in range(pp, C):
                    u[a0:a0 + W, t * W:(t + 1) * W] = gb[t, a0:a0 + W, :]
                if pp:
                    u[a0:a0 + W, a0:] = u[a0:a0 + W, a0:] - lax.dot_general(
                        u[0:a0, a0:a0 + W], u[0:a0, a0:], TN, precision=HI, preferred_element_type=f32)
        aug[:, 0:W] = u[pl.ds(base, W), pl.ds(base, W)]
        aug[:, W:] = jnp.where(pr == pc, 1.0, 0.0).astype(f32)
        panel_factor(aug, upan)
        u[pl.ds(base, W), pl.ds(base, W)] = jnp.where(pr <= pc, upan[:, 0:W], 0.0)
        for pp in range(C - 1):
            @pl.when(p == pp)
            def _():
                a0, a1 = pp * W, (pp + 1) * W
                linv = jnp.where(pr >= pc, upan[:, W:], 0.0)
                u[a0:a1, a1:] = jnp.dot(linv, u[a0:a1, a1:], precision=HI, preferred_element_type=f32)
        return 0

    lax.fori_loop(0, C, panel, 0)
    here = pl.ds(pl.multiple_of(col * W, W), W)
    for j in range(C):
        fac_ref[j * W:(j + 1) * W, :] = jnp.transpose(u[here, j * W:(j + 1) * W])

    waits(w_req, False)
    waits(w_sec, False)
    waits(w_ans, False)
    for c in started:
        c.wait_send()
    for j in xpeers:
        w_x(j).wait_send()

    def left(p):
        @pl.when(p <= col)
        def _():
            @pl.when(mx == p // per)
            def _():
                for j in xpeers:
                    c_xg(p, j).wait_send()
            for k in range(len(ypeers)):
                c_cg(p, k).wait_send()
            c_fw(col, p).wait_send()
        for s in ypeers:
            @pl.when(p <= s)
            def _():
                c_fw(s, p).wait_send()
    each(left, 0, C)
    for k in range(1, Z):
        w_z(zpeers(k)).wait_send()
        w_zg(zpeers(k)).wait_send()


def exchange(a, signs, blocks, offs, X, Z, C):
    rows, W = a.shape
    D = X * Z
    S = offs.shape[0]
    cap = max(2, 2 * S // D)
    rb = rows // D
    R = D * cap
    q = C * W // X
    V = pltpu.VMEM
    dma = pltpu.SemaphoreType.DMA
    return pl.pallas_call(
        functools.partial(exchange_kernel, X, Z, C, 1.0 / math.sqrt(D * rows), float(D * S)),
        out_shape=(jax.ShapeDtypeStruct((C * W, W), f32), jax.ShapeDtypeStruct((S, W), f32)),
        in_specs=[pl.BlockSpec(memory_space=V)] * 4,
        out_specs=(pl.BlockSpec(memory_space=V), pl.BlockSpec(memory_space=V)),
        scratch_shapes=[
            V((rows, W), f32), V((rows, W), f32), V((rows + 8, W), f32),
            V((D, 1, 128), jnp.int32), V((D, 1, 128), jnp.int32), pltpu.SMEM((D, 1, 128), jnp.int32),
            V((S // 128, 1, 128), jnp.int32), pltpu.SMEM((S // 128, 1, 128), jnp.int32),
            V((R, W), f32), V((R, W), f32), V((C, R, W), f32),
            V((C * W, W), f32), V((X, q, W), f32), V((Z, q // Z, W), f32), V((Z, q // Z, W), f32),
            V((C, C * W, W), f32), V((C * W, C * W), f32), V((W, 2 * W), f32), V((W, 2 * W), f32),
            dma((D,)), dma((D,)), dma((D,)), dma((D,)), dma((D,)), dma((D,)),
            dma((C, 1 + C // 2)), dma((C,)), dma((X,)), dma((X,)), dma((Z,)), dma((Z,)),
            dma((Z,)), dma((Z,)), dma((C, X)), dma((C,)), dma((C, C // 2)), dma((C, C)), dma((C, C)), dma((2,)),
        ],
        compiler_params=pltpu.CompilerParams(collective_id=0, has_side_effects=True, vmem_limit_bytes=48 * 2**20),
        name="exchange",
    )(a, signs.reshape(rows // 128, 128), blocks, offs.reshape(S // 128, 128))


def solution(mesh):
    x_size, z_size, c_size = 4, mesh.shape["row"] // 4, mesh.shape["col"]

    def shards(matrix, row_signs, sample_block, sample_offset):
        factor, sketch = exchange(matrix, row_signs, sample_block, sample_offset, x_size, z_size, c_size)
        return sketch, factor

    placed = (P("row", "col"), P("row"), P("row", None), P("row"))
    return jax.shard_map(
        shards,
        mesh=mesh,
        in_specs=placed,
        out_specs=(P("row", "col"), P(None, "col")),
        check_vma=False,
    )
```

```python
import functools
import math

import jax
import jax.numpy as jnp
from jax import lax
from jax.experimental import pallas as pl
from jax.experimental.pallas import tpu as pltpu
from jax.sharding import PartitionSpec as P

f32, bf16 = jnp.float32, jnp.bfloat16
TN = (((0,), (0,)), ((), ()))
HI = lax.Precision.HIGHEST


def butterflies(v):
    n, step = len(v), 1
    while step < n:
        v = [v[i] + v[i + step] if not i & step else v[i - step] - v[i] for i in range(n)]
        step *= 2
    return v


def mix_pass(src, dst, rows, low, bits, scale=None):
    n, stride = 1 << bits, 1 << low
    tiles = stride // 8
    groups = rows // (n * stride)

    def body(t, _):
        g, j = t // tiles, t % tiles
        base = g * (n * stride) + j * 8
        v = [src[pl.ds(pl.multiple_of(base + i * stride, 8), 8), :] for i in range(n)]
        v = butterflies(v)
        for i in range(n):
            dst[pl.ds(pl.multiple_of(base + i * stride, 8), 8), :] = v[i] if scale is None else v[i] * scale
        return 0

    lax.fori_loop(0, groups * tiles, body, 0, unroll=2 if groups * tiles % 2 == 0 else 1)


PAN = 128
BLK = 16


def panel_factor(aug, upan):
    wide = 2 * PAN
    lanes = wide // PAN
    cur = [[aug[8 * r:8 * r + 8, h * PAN:(h + 1) * PAN] for h in range(lanes)] for r in range(BLK // 8)]
    nblk, sub = PAN // BLK, BLK // 8
    for t in range(nblk):
        lo = t * BLK
        last = t == nblk - 1
        C = [[jnp.broadcast_to(cur[r][0][:, lo + k:lo + k + 1], (8, PAN)) for r in range(sub)] for k in range(BLK)]
        if not last:
            xt = jnp.transpose(jnp.concatenate([cur[r][0] for r in range(sub)], axis=0))[lo + BLK:lo + 2 * BLK, :]
            N = [[jnp.broadcast_to(xt[8 * r:8 * r + 8, k:k + 1], (8, PAN)) for r in range(sub)] for k in range(BLK)]
            nxt = aug[lo + BLK:lo + 2 * BLK, :]
            if t > 0:
                done = upan[0:lo, :]
                nxt = nxt - lax.dot_general(done[:, lo + BLK:lo + 2 * BLK], done, TN,
                                            precision=HI, preferred_element_type=f32)
            acc = [[None] * lanes for _ in range(sub)]
        R = cur
        for k in range(BLK):
            rs = lax.rsqrt(C[k][k // 8][k % 8:k % 8 + 1, :])
            u = [R[k // 8][h][k % 8:k % 8 + 1, :] * rs for h in range(lanes)]
            for h in range(lanes):
                upan[lo + k:lo + k + 1, h * PAN:(h + 1) * PAN] = u[h]
            first = (k + 1) // 8
            L = [C[k][r] * rs if r >= first else None for r in range(sub)]
            Nl = [N[k][r] * rs for r in range(sub)] if not last else None
            for c in range(k + 1, BLK):
                m = L[c // 8][c % 8:c % 8 + 1, :]
                for r in range(c // 8, sub):
                    C[c][r] = C[c][r] - L[r] * m
                if not last:
                    for r in range(sub):
                        N[c][r] = N[c][r] - Nl[r] * m
            for h in range(lanes):
                for r in range(first, sub):
                    R[r][h] = R[r][h] - L[r] * u[h]
                if not last:
                    for r in range(sub):
                        acc[r][h] = Nl[r] * u[h] if acc[r][h] is None else acc[r][h] + Nl[r] * u[h]
        if not last:
            cur = [[nxt[8 * r:8 * r + 8, h * PAN:(h + 1) * PAN] - acc[r][h] for h in range(lanes)] for r in range(sub)]


def exchange_kernel(X, Z, C, norm, samples,
                    a_ref, sign_ref, blk_ref, off_ref,
                    fac_ref, sk_ref,
                    v, sign, pos, recv, table, req, reqx, reqr, reqs, own, owns, ans, ansz, ret, xall, part, xr, zs, zr,
                    gb, u, aug, upan,
                    s_rx, r_rx, s_rz, r_rz, s_sec, r_sec, s_az, r_az, s_ax, r_ax, s_col, r_col, s_x, r_x, s_z, r_z,
                    s_zg, r_zg, s_xg, r_xg, s_cg, s_fw, s_rl, r_cg, l_sem):
    D = X * Z
    rows, W = v.shape
    rb = rows // D
    cap = ret.shape[0] // D
    SR = blk_ref.shape[0]
    S = SR * 128
    me, col = lax.axis_index("row"), lax.axis_index("col")
    mx, mz = me // Z, me % Z
    sib = col + 1 - 2 * (col % 2)

    def rcopy(src, dst, ss, rs, row=None, c=None):
        dev = {"row": row} if c is None else {"col": c}
        return pltpu.make_async_remote_copy(src_ref=src, dst_ref=dst, send_sem=ss, recv_sem=rs,
                                            device_id=dev, device_id_type=pl.DeviceIdType.MESH)

    bar = pltpu.get_barrier_semaphore()

    def greet(k, _):
        pl.semaphore_signal(bar, inc=1, device_id={"row": lax.rem(me + k, D)}, device_id_type=pl.DeviceIdType.MESH)
        return 0
    lax.fori_loop(1, D, greet, 0)
    ypeers = [lax.rem(col + 2 * k, C) for k in range(1, C // 2)]
    for c in [sib] + ypeers:
        pl.semaphore_signal(bar, inc=1, device_id={"col": c}, device_id_type=pl.DeviceIdType.MESH)

    fetch = [pltpu.make_async_copy(src, dst, l_sem.at[2 + k]) for k, (src, dst) in enumerate(
        [(blk_ref, pos.at[0]), (off_ref, pos.at[1]), (sign_ref, sign), (a_ref, v)])]
    for c in fetch:
        c.start()
    nb = rows // 128
    fetch[2].wait()
    fetch[3].wait()
    st = jnp.transpose(jnp.concatenate([sign[...].astype(f32), jnp.zeros((128 - nb, 128), f32)], axis=0))
    for j in range(nb):
        v[j * 128:(j + 1) * 128, :] = v[j * 128:(j + 1) * 128, :] * jnp.broadcast_to(st[:, j:j + 1], (128, W))

    def low_bits(g, _):
        base = pl.multiple_of(g * 64, 64)
        w = butterflies([v[pl.ds(base + k, 8, stride=8), :] for k in range(8)])
        for k in range(8):
            v[pl.ds(base + k, 8, stride=8), :] = w[k]
        return 0
    lax.fori_loop(0, rows // 64, low_bits, 0, unroll=2)
    left, low = rows.bit_length() - 1 - 3, 3
    while left:
        b = min(3, left)
        mix_pass(v, v, rows, low, b)
        low, left = low + b, left - b

    pl.semaphore_wait(bar, D - 1 + 1 + len(ypeers))

    def peer_of(k):
        return lax.rem(me + jnp.where(k % 2 == 1, (k + 1) // 2, D - k // 2), D)

    def sends(fn):
        def go(k, _):
            fn(peer_of(k)).start()
            return 0
        lax.fori_loop(1, D, go, 0)

    xpeers = [lax.rem(mx + k, X) for k in range(1, X)]
    zpeers = lambda k: lax.rem(mz + k, Z)
    c_rx = lambda j: rcopy(req.at[j], reqx.at[mx], s_rx.at[j], r_rx.at[mx], row=j * Z + mz)
    w_rx = lambda j: rcopy(req.at[j], reqx.at[j], s_rx.at[j], r_rx.at[j], row=j * Z + mz)
    c_rz = lambda j: rcopy(reqx.at[:, j], reqr.at[:, mz], s_rz.at[j], r_rz.at[mz], row=mx * Z + j)
    w_rz = lambda j: rcopy(reqx.at[:, j], reqr.at[:, j], s_rz.at[j], r_rz.at[j], row=mx * Z + j)
    sec = lambda j: v.at[pl.ds(pl.multiple_of(j * rb, rb), rb), :]
    got = lambda j: recv.at[pl.ds(pl.multiple_of(j * rb, rb), rb), :]
    c_sec = lambda j: rcopy(sec(j), got(me), s_sec.at[0], r_sec.at[0], row=j)
    others = pl.ds(0, (D - 1) * rb)
    all_sec = rcopy(v.at[others, :], recv.at[others, :], s_sec.at[0], r_sec.at[0], row=lax.rem(me + 1, D))
    sends(c_sec)
    fetch[0].wait()
    fetch[1].wait()

    both = jnp.transpose(jnp.concatenate(
        [pos[0].astype(f32), pos[1].astype(f32), jnp.zeros((128 - 2 * SR, 128), f32)], axis=0))
    blocks, offc = [jnp.concatenate([both[:, k:k + 1] for k in range(b, b + SR)], axis=0) for b in (0, SR)]
    lane = lax.broadcasted_iota(jnp.int32, (S, 128), 1)
    onehot = (blocks == lane.astype(f32)).astype(f32)
    ri = lax.broadcasted_iota(jnp.int32, (S, S), 0)
    ci = lax.broadcasted_iota(jnp.int32, (S, S), 1)
    before = jnp.dot((ci < ri).astype(bf16), onehot.astype(bf16), preferred_element_type=f32)
    slot = jnp.sum(before * onehot, axis=1, keepdims=True)
    val = jnp.where(lane.astype(f32) == slot, offc - float(rows), 0.0)
    wanted = lax.dot_general(onehot, val, TN, precision=HI, preferred_element_type=f32) + float(rows)
    wanted = wanted.astype(jnp.int32)
    for j in range(D):
        req[j // Z, j % Z] = wanted[j:j + 1, :]
    place = blocks * float(cap) + slot
    for k in range(S // 128):
        t = jnp.transpose(jnp.broadcast_to(place[k * 128:(k + 1) * 128, :], (128, 128)))
        own[k] = t[0:1, :].astype(jnp.int32)
    oc = pltpu.make_async_copy(own, owns, l_sem.at[0])
    oc.start()

    for j in xpeers:
        c_rx(j).start()
    reqx[mx] = req[mx]
    for j in xpeers:
        w_rx(j).wait_recv()
    for k in range(1, Z):
        c_rz(zpeers(k)).start()
    reqr[:, mz] = reqx[:, mz]
    recv[pl.ds(pl.multiple_of(me * rb, rb), rb), :] = v[pl.ds(pl.multiple_of(me * rb, rb), rb), :]
    table[rows:rows + 8, :] = jnp.zeros((8, W), f32)
    for k in range(1, Z):
        w_rz(zpeers(k)).wait_recv()
    rc = pltpu.make_async_copy(reqr, reqs, l_sem.at[1])
    rc.start()
    rc.wait()
    oc.wait()
    all_sec.wait_recv()

    lowb = rb.bit_length() - 1
    left, low, first = D.bit_length() - 1, lowb, True
    while left:
        b = min(3, left)
        left -= b
        mix_pass(recv if first else table, table, rows, low, b, norm if left == 0 else None)
        low, first = low + b, False

    R = D * cap
    for x in range(X):
        def answer(z, _, x=x):
            for c in range(cap):
                ans[x, pl.ds(z * cap + c, 1), :] = table[pl.ds(jnp.clip(reqs[x, z, 0, c], 0, rows), 1), :]
            return 0
        lax.fori_loop(0, Z, answer, 0, unroll=2 if Z % 2 == 0 else 1)
        xall[col, x * Z * cap:(x + 1) * Z * cap, :] = ans[x]

    half = R // 2
    up, down = lax.rem(col + 2, C), lax.rem(col + C - 2, C)

    def c_col(s, h, t):
        ref = xall.at[s, pl.ds(h * half, half), :]
        return rcopy(ref, ref, s_col.at[s, h, t], r_col.at[s, h], c=(sib, up, down)[t])
    started = []

    def go(s, h, t):
        started.append(c_col(s, h, t))
        started[-1].start()
    ring = C > 4
    far = lax.rem(col + 4, C)
    go(col, 0, 2)
    go(col, 1, 1 if ring else 2)
    go(col, 0, 0)
    go(col, 1, 0)
    if ring:
        go(col, 1, 2)
        go(col, 0, 1)
    slots = lambda ref, z: ref.at[:, pl.ds(pl.multiple_of(z * cap, 8), cap), :]
    c_az = lambda j: rcopy(slots(ans, j), slots(ansz, mz), s_az.at[j], r_az.at[mz], row=mx * Z + j)
    w_az = lambda j: rcopy(slots(ans, j), slots(ansz, j), s_az.at[j], r_az.at[j], row=mx * Z + j)
    flat = lambda x: ret.at[pl.ds(pl.multiple_of(x * Z * cap, 8), Z * cap), :]
    c_ax = lambda j: rcopy(ansz.at[j], flat(mx), s_ax.at[j], r_ax.at[mx], row=j * Z + mz)
    w_ax = lambda j: rcopy(ansz.at[j], flat(j), s_ax.at[j], r_ax.at[j], row=j * Z + mz)

    mine = jnp.transpose(xall[col])

    def block(s):
        part[pl.ds(pl.multiple_of(s * W, W), W), :] = jnp.transpose(
            jnp.dot(mine, xall[s], precision=HI, preferred_element_type=f32))
    block(col)
    if ring:
        c_col(up, 0, 0).wait_recv()
        go(up, 0, 2)
        go(up, 0, 0)
        c_col(down, 1, 0).wait_recv()
        go(down, 1, 1)
        go(down, 1, 0)
    if ring:
        c_col(up, 1, 0).wait_recv()
        go(up, 1, 0)
        block(up)
        c_col(down, 0, 0).wait_recv()
        go(down, 0, 0)
        block(down)
        for h in range(2):
            c_col(far, h, 0).wait_recv()
            go(far, h, 0)
        block(far)
    else:
        for h in range(2):
            c_col(up, h, 0).wait_recv()
            go(up, h, 0)
        block(up)
    for k in (0, 1, 3, 2) if ring else (0, 1):
        s = lax.rem(sib + 2 * k, C)
        for h in range(2):
            c_col(s, h, 0).wait_recv()
        block(s)

    q = C * W // X
    xs = lambda j: part.at[pl.ds(pl.multiple_of(j * q, q), q), :]
    c_x = lambda j: rcopy(xs(j), xr.at[mx], s_x.at[j], r_x.at[mx], row=j * Z + mz)
    w_x = lambda j: rcopy(xs(j), xr.at[j], s_x.at[j], r_x.at[j], row=j * Z + mz)
    for j in xpeers:
        c_x(j).start()
    xr[mx] = part[pl.ds(pl.multiple_of(mx * q, q), q), :]

    for j in xpeers:
        w_x(j).wait_recv()
    acc = xr[0]
    for j in range(1, X):
        acc = acc + xr[j]
    e = q // Z
    zs[...] = acc.reshape(Z, e, W)
    c_z = lambda j: rcopy(zs.at[j], zr.at[mz], s_z.at[j], r_z.at[mz], row=mx * Z + j)
    w_z = lambda j: rcopy(zs.at[j], zr.at[j], s_z.at[j], r_z.at[j], row=mx * Z + j)
    for k in range(1, Z):
        c_z(zpeers(k)).start()
    zr[mz] = zs[mz]
    for k in range(1, Z):
        w_z(zpeers(k)).wait_recv()
    acc = zr[0]
    for j in range(1, Z):
        acc = acc + zr[j]
    gb[col, pl.ds(pl.multiple_of(mx * q + mz * e, e), e), :] = acc / samples
    ze = lambda j: gb.at[col, pl.ds(pl.multiple_of(mx * q + j * e, e), e), :]
    c_zg = lambda j: rcopy(ze(mz), ze(mz), s_zg.at[j], r_zg.at[mz], row=mx * Z + j)
    w_zg = lambda j: rcopy(ze(j), ze(j), s_zg.at[j], r_zg.at[j], row=mx * Z + j)
    for k in range(1, Z):
        c_zg(zpeers(k)).start()
    for k in range(1, Z):
        w_zg(zpeers(k)).wait_recv()
    per = C // X
    gblk = lambda s, p: gb.at[s, pl.ds(pl.multiple_of(p * W, W), W), :]
    c_xg = lambda p, j: rcopy(gblk(col, p), gblk(col, p), s_xg.at[p, j], r_xg.at[p], row=j * Z + mz)
    c_cg = lambda p, k: rcopy(gblk(col, p), gblk(col, p), s_cg.at[p, k], r_cg.at[col, p], c=(up, down)[k])
    c_fw = lambda s, p: rcopy(gblk(s, p), gblk(s, p), s_fw.at[s, p], r_cg.at[s, p], c=sib)
    c_rl = lambda s, p, k: rcopy(gblk(s, p), gblk(s, p), s_rl.at[p], r_cg.at[s, p], c=(up, down)[k])
    sides = [(up, 1), (down, 0)] if ring else [(up, 1)]

    def along_x(p):
        @pl.when((mx == p // per) & (p <= col))
        def _():
            for j in xpeers:
                c_xg(p, j).start()

    def own_block(p):
        @pl.when(p <= col)
        def _():
            @pl.when(mx != p // per)
            def _():
                c_xg(p, mx).wait_recv()
            for k in range(len(sides)):
                c_cg(p, k).start()
            c_fw(col, p).start()

    def relayed(p, do):
        for b, (s, k) in enumerate(sides):
            @pl.when(p <= s)
            def _():
                do(s, p, k, b)

    def relay(p):
        def do(s, p, k, b):
            c_fw(s, p).wait_recv()
            if ring:
                @pl.when(p % 2 == b)
                def _():
                    c_rl(s, p, k).start()
            c_fw(s, p).start()
        relayed(p, do)

    def opposite(p):
        if ring:
            @pl.when(p <= far)
            def _():
                c_fw(far, p).wait_recv()
                c_fw(far, p).start()

    def arrived(p):
        for k in range(C // 2):
            s = lax.rem(sib + 2 * k, C)

            @pl.when(p <= s)
            def _():
                c_fw(s, p).wait_recv()

    def each(fn, lo, hi):
        lax.fori_loop(lo, hi, lambda p, _: (fn(p), 0)[1], 0)
    each(along_x, 0, C)
    own_block(0)
    own_block(1)
    u[...] = jnp.zeros_like(u)
    relay(0)
    own_block(2)
    relay(1)
    opposite(0)

    pr = lax.broadcasted_iota(jnp.int32, (W, W), 0)
    pc = lax.broadcasted_iota(jnp.int32, (W, W), 1)

    def panel(p, _):
        for ahead, fn in ((3, own_block), (2, relay), (1, opposite)):
            @pl.when(p + ahead < C)
            def _():
                fn(p + ahead)
        arrived(p)
        base = pl.multiple_of(p * W, W)
        for pp in range(C):
            @pl.when(p == pp)
            def _():
                a0 = pp * W
                for t in range(pp, C):
                    u[a0:a0 + W, t * W:(t + 1) * W] = gb[t, a0:a0 + W, :]
                if pp:
                    u[a0:a0 + W, a0:] = u[a0:a0 + W, a0:] - lax.dot_general(
                        u[0:a0, a0:a0 + W], u[0:a0, a0:], TN, precision=HI, preferred_element_type=f32)
        aug[:, 0:W] = u[pl.ds(base, W), pl.ds(base, W)]
        aug[:, W:] = jnp.where(pr == pc, 1.0, 0.0).astype(f32)
        panel_factor(aug, upan)
        u[pl.ds(base, W), pl.ds(base, W)] = jnp.where(pr <= pc, upan[:, 0:W], 0.0)
        for pp in range(C - 1):
            @pl.when(p == pp)
            def _():
                a0, a1 = pp * W, (pp + 1) * W
                linv = jnp.where(pr >= pc, upan[:, W:], 0.0)
                u[a0:a1, a1:] = jnp.dot(linv, u[a0:a1, a1:], precision=HI, preferred_element_type=f32)

        @pl.when(p == 0)
        def _():
            for k in range(1, Z):
                c_az(zpeers(k)).start()
            ansz[:, pl.ds(pl.multiple_of(mz * cap, 8), cap), :] = ans[:, pl.ds(pl.multiple_of(mz * cap, 8), cap), :]

        @pl.when(p == C // 2)
        def _():
            for k in range(1, Z):
                w_az(zpeers(k)).wait_recv()
            for j in xpeers:
                c_ax(j).start()
            ret[pl.ds(pl.multiple_of(mx * Z * cap, 8), Z * cap), :] = ansz[mx]

        @pl.when(p == C - 2)
        def _():
            for j in xpeers:
                w_ax(j).wait_recv()

            def keep(t, _):
                k, first = t // 16, t % 16
                for i in range(8):
                    at = jnp.clip(owns[k, 0, first * 8 + i], 0, R - 1)
                    sk_ref[pl.ds(t * 8 + i, 1), :] = ret[pl.ds(at, 1), :]
                return 0
            lax.fori_loop(0, S // 8, keep, 0)
        return 0

    lax.fori_loop(0, C, panel, 0)
    here = pl.ds(pl.multiple_of(col * W, W), W)
    for j in range(C):
        fac_ref[j * W:(j + 1) * W, :] = jnp.transpose(u[here, j * W:(j + 1) * W])

    all_sec.wait_send()
    for j in xpeers:
        w_rx(j).wait_send()
        w_ax(j).wait_send()
    for k in range(1, Z):
        w_rz(zpeers(k)).wait_send()
        w_az(zpeers(k)).wait_send()
    for c in started:
        c.wait_send()
    for j in xpeers:
        w_x(j).wait_send()

    def left(p):
        @pl.when(p <= col)
        def _():
            @pl.when(mx == p // per)
            def _():
                for j in xpeers:
                    c_xg(p, j).wait_send()
            for k in range(len(sides)):
                c_cg(p, k).wait_send()
            c_fw(col, p).wait_send()

        def do(s, p, k, b):
            if ring:
                @pl.when(p % 2 == b)
                def _():
                    c_rl(s, p, k).wait_send()
            c_fw(s, p).wait_send()
        relayed(p, do)
        if ring:
            @pl.when(p <= far)
            def _():
                c_fw(far, p).wait_send()
    each(left, 0, C)
    for k in range(1, Z):
        w_z(zpeers(k)).wait_send()
        w_zg(zpeers(k)).wait_send()


def exchange(a, signs, blocks, offs, X, Z, C):
    rows, W = a.shape
    D = X * Z
    S = offs.shape[0]
    cap = max(2, 2 * S // D)
    rb = rows // D
    R = D * cap
    q = C * W // X
    V = pltpu.VMEM
    dma = pltpu.SemaphoreType.DMA
    return pl.pallas_call(
        functools.partial(exchange_kernel, X, Z, C, 1.0 / math.sqrt(D * rows), float(D * S)),
        out_shape=(jax.ShapeDtypeStruct((C * W, W), f32), jax.ShapeDtypeStruct((S, W), f32)),
        in_specs=[pl.BlockSpec(memory_space=pl.ANY)] * 4,
        out_specs=(pl.BlockSpec(memory_space=V), pl.BlockSpec(memory_space=V)),
        scratch_shapes=[
            V((rows, W), f32), V((rows // 128, 128), jnp.int32), V((2, S // 128, 128), jnp.int32),
            V((rows, W), f32), V((rows + 8, W), f32),
            V((X, Z, 1, 128), jnp.int32), V((X, Z, 1, 128), jnp.int32), V((X, Z, 1, 128), jnp.int32),
            pltpu.SMEM((X, Z, 1, 128), jnp.int32),
            V((S // 128, 1, 128), jnp.int32), pltpu.SMEM((S // 128, 1, 128), jnp.int32),
            V((X, Z * cap, W), f32), V((X, Z * cap, W), f32), V((R, W), f32), V((C, R, W), f32),
            V((C * W, W), f32), V((X, q, W), f32), V((Z, q // Z, W), f32), V((Z, q // Z, W), f32),
            V((C, C * W, W), f32), V((C * W, C * W), f32), V((W, 2 * W), f32), V((W, 2 * W), f32),
            dma((X,)), dma((X,)), dma((Z,)), dma((Z,)), dma((1,)), dma((1,)), dma((Z,)), dma((Z,)), dma((X,)), dma((X,)),
            dma((C, 2, 3)), dma((C, 2)), dma((X,)), dma((X,)), dma((Z,)), dma((Z,)),
            dma((Z,)), dma((Z,)), dma((C, X)), dma((C,)), dma((C, 2)), dma((C, C)), dma((C,)), dma((C, C)), dma((6,)),
        ],
        compiler_params=pltpu.CompilerParams(collective_id=0, has_side_effects=True, vmem_limit_bytes=60 * 2**20),
        name="exchange",
    )(a, signs.reshape(rows // 128, 128), blocks.reshape(S // 128, 128), offs.reshape(S // 128, 128))


def solution(mesh):
    x_size, z_size, c_size = 4, mesh.shape["row"] // 4, mesh.shape["col"]

    def shards(matrix, row_signs, sample_block, sample_offset):
        factor, sketch = exchange(matrix, row_signs, sample_block, sample_offset, x_size, z_size, c_size)
        return sketch, factor

    placed = (P("row", "col"), P("row"), P("row", None), P("row"))
    return jax.shard_map(
        shards,
        mesh=mesh,
        in_specs=placed,
        out_specs=(P("row", "col"), P(None, "col")),
        check_vma=False,
    )
```

```python
import functools
import math

import jax
import jax.numpy as jnp
from jax import lax
from jax.experimental import pallas as pl
from jax.experimental.pallas import tpu as pltpu
from jax.sharding import PartitionSpec as P

f32, bf16 = jnp.float32, jnp.bfloat16
TN = (((0,), (0,)), ((), ()))
HI = lax.Precision.HIGHEST


def butterflies(v):
    n, step = len(v), 1
    while step < n:
        v = [v[i] + v[i + step] if not i & step else v[i - step] - v[i] for i in range(n)]
        step *= 2
    return v


def mix_pass(src, dst, rows, low, bits, scale=None):
    n, stride = 1 << bits, 1 << low
    tiles = stride // 8
    groups = rows // (n * stride)

    def body(t, _):
        g, j = t // tiles, t % tiles
        base = g * (n * stride) + j * 8
        v = [src[pl.ds(pl.multiple_of(base + i * stride, 8), 8), :] for i in range(n)]
        v = butterflies(v)
        for i in range(n):
            dst[pl.ds(pl.multiple_of(base + i * stride, 8), 8), :] = v[i] if scale is None else v[i] * scale
        return 0

    lax.fori_loop(0, groups * tiles, body, 0, unroll=2 if groups * tiles % 2 == 0 else 1)


PAN = 128
BLK = 16


def panel_factor(aug, upan):
    wide = 2 * PAN
    lanes = wide // PAN
    cur = [[aug[8 * r:8 * r + 8, h * PAN:(h + 1) * PAN] for h in range(lanes)] for r in range(BLK // 8)]
    nblk, sub = PAN // BLK, BLK // 8
    for t in range(nblk):
        lo = t * BLK
        last = t == nblk - 1
        C = [[jnp.broadcast_to(cur[r][0][:, lo + k:lo + k + 1], (8, PAN)) for r in range(sub)] for k in range(BLK)]
        if not last:
            xt = jnp.transpose(jnp.concatenate([cur[r][0] for r in range(sub)], axis=0))[lo + BLK:lo + 2 * BLK, :]
            N = [[jnp.broadcast_to(xt[8 * r:8 * r + 8, k:k + 1], (8, PAN)) for r in range(sub)] for k in range(BLK)]
            nxt = aug[lo + BLK:lo + 2 * BLK, :]
            if t > 0:
                done = upan[0:lo, :]
                nxt = nxt - lax.dot_general(done[:, lo + BLK:lo + 2 * BLK], done, TN,
                                            precision=HI, preferred_element_type=f32)
            acc = [[None] * lanes for _ in range(sub)]
        R = cur
        for k in range(BLK):
            rs = lax.rsqrt(C[k][k // 8][k % 8:k % 8 + 1, :])
            u = [R[k // 8][h][k % 8:k % 8 + 1, :] * rs for h in range(lanes)]
            for h in range(lanes):
                upan[lo + k:lo + k + 1, h * PAN:(h + 1) * PAN] = u[h]
            first = (k + 1) // 8
            L = [C[k][r] * rs if r >= first else None for r in range(sub)]
            Nl = [N[k][r] * rs for r in range(sub)] if not last else None
            for c in range(k + 1, BLK):
                m = L[c // 8][c % 8:c % 8 + 1, :]
                for r in range(c // 8, sub):
                    C[c][r] = C[c][r] - L[r] * m
                if not last:
                    for r in range(sub):
                        N[c][r] = N[c][r] - Nl[r] * m
            for h in range(lanes):
                for r in range(first, sub):
                    R[r][h] = R[r][h] - L[r] * u[h]
                if not last:
                    for r in range(sub):
                        acc[r][h] = Nl[r] * u[h] if acc[r][h] is None else acc[r][h] + Nl[r] * u[h]
        if not last:
            cur = [[nxt[8 * r:8 * r + 8, h * PAN:(h + 1) * PAN] - acc[r][h] for h in range(lanes)] for r in range(sub)]


def exchange_kernel(X, Z, C, norm, samples,
                    a_ref, sign_ref, blk_ref, off_ref,
                    fac_ref, sk_ref,
                    v, sign, pos, recv, table, req, reqx, reqr, reqs, own, owns, ans, ansz, ret, xall, part, xr, zs, zr,
                    gb, u, aug, upan,
                    s_rx, r_rx, s_rz, r_rz, s_sec, r_sec, s_az, r_az, s_ax, r_ax, s_col, r_col, s_x, r_x, s_z, r_z,
                    s_zg, r_zg, s_xg, r_xg, s_cg, s_fw, r_cg, l_sem):
    D = X * Z
    rows, W = v.shape
    rb = rows // D
    cap = ret.shape[0] // D
    SR = blk_ref.shape[0]
    S = SR * 128
    me, col = lax.axis_index("row"), lax.axis_index("col")
    mx, mz = me // Z, me % Z
    sib = col + 1 - 2 * (col % 2)

    def rcopy(src, dst, ss, rs, row=None, c=None):
        dev = {"row": row} if c is None else {"col": c}
        return pltpu.make_async_remote_copy(src_ref=src, dst_ref=dst, send_sem=ss, recv_sem=rs,
                                            device_id=dev, device_id_type=pl.DeviceIdType.MESH)

    bar = pltpu.get_barrier_semaphore()

    def greet(k, _):
        pl.semaphore_signal(bar, inc=1, device_id={"row": lax.rem(me + k, D)}, device_id_type=pl.DeviceIdType.MESH)
        return 0
    lax.fori_loop(1, D, greet, 0)
    ypeers = [lax.rem(col + 2 * k, C) for k in range(1, C // 2)]
    for c in [sib] + ypeers:
        pl.semaphore_signal(bar, inc=1, device_id={"col": c}, device_id_type=pl.DeviceIdType.MESH)

    fetch = [pltpu.make_async_copy(src, dst, l_sem.at[2 + k]) for k, (src, dst) in enumerate(
        [(blk_ref, pos.at[0]), (off_ref, pos.at[1]), (sign_ref, sign), (a_ref, v)])]
    for c in fetch:
        c.start()
    nb = rows // 128
    fetch[2].wait()
    fetch[3].wait()
    st = jnp.transpose(jnp.concatenate([sign[...].astype(f32), jnp.zeros((128 - nb, 128), f32)], axis=0))
    for j in range(nb):
        v[j * 128:(j + 1) * 128, :] = v[j * 128:(j + 1) * 128, :] * jnp.broadcast_to(st[:, j:j + 1], (128, W))

    def low_bits(g, _):
        base = pl.multiple_of(g * 64, 64)
        w = butterflies([v[pl.ds(base + k, 8, stride=8), :] for k in range(8)])
        for k in range(8):
            v[pl.ds(base + k, 8, stride=8), :] = w[k]
        return 0
    lax.fori_loop(0, rows // 64, low_bits, 0, unroll=2)
    left, low = rows.bit_length() - 1 - 3, 3
    while left:
        b = min(3, left)
        mix_pass(v, v, rows, low, b)
        low, left = low + b, left - b

    pl.semaphore_wait(bar, D - 1 + 1 + len(ypeers))

    def peer_of(k):
        return lax.rem(me + jnp.where(k % 2 == 1, (k + 1) // 2, D - k // 2), D)

    def sends(fn, lo, hi):
        def go(k, _):
            fn(peer_of(k)).start()
            return 0
        lax.fori_loop(lo, hi, go, 0)

    xpeers = [lax.rem(mx + k, X) for k in range(1, X)]
    zpeers = lambda k: lax.rem(mz + k, Z)
    c_rx = lambda j: rcopy(req.at[j], reqx.at[mx], s_rx.at[j], r_rx.at[mx], row=j * Z + mz)
    w_rx = lambda j: rcopy(req.at[j], reqx.at[j], s_rx.at[j], r_rx.at[j], row=j * Z + mz)
    c_rz = lambda j: rcopy(reqx.at[:, j], reqr.at[:, mz], s_rz.at[j], r_rz.at[mz], row=mx * Z + j)
    w_rz = lambda j: rcopy(reqx.at[:, j], reqr.at[:, j], s_rz.at[j], r_rz.at[j], row=mx * Z + j)
    sec = lambda j: v.at[pl.ds(pl.multiple_of(j * rb, rb), rb), :]
    got = lambda j: recv.at[pl.ds(pl.multiple_of(j * rb, rb), rb), :]
    c_sec = lambda j: rcopy(sec(j), got(me), s_sec.at[0], r_sec.at[0], row=j)
    others = pl.ds(0, (D - 1) * rb)
    all_sec = rcopy(v.at[others, :], recv.at[others, :], s_sec.at[0], r_sec.at[0], row=lax.rem(me + 1, D))
    sends(c_sec, 1, D // 4)
    fetch[0].wait()
    fetch[1].wait()

    both = jnp.transpose(jnp.concatenate(
        [pos[0].astype(f32), pos[1].astype(f32), jnp.zeros((128 - 2 * SR, 128), f32)], axis=0))
    blocks, offc = [jnp.concatenate([both[:, k:k + 1] for k in range(b, b + SR)], axis=0) for b in (0, SR)]
    lane = lax.broadcasted_iota(jnp.int32, (S, 128), 1)
    onehot = (blocks == lane.astype(f32)).astype(f32)
    ri = lax.broadcasted_iota(jnp.int32, (S, S), 0)
    ci = lax.broadcasted_iota(jnp.int32, (S, S), 1)
    before = jnp.dot((ci < ri).astype(bf16), onehot.astype(bf16), preferred_element_type=f32)
    slot = jnp.sum(before * onehot, axis=1, keepdims=True)
    val = jnp.where(lane.astype(f32) == slot, offc - float(rows), 0.0)
    wanted = lax.dot_general(onehot, val, TN, precision=HI, preferred_element_type=f32) + float(rows)
    wanted = wanted.astype(jnp.int32)
    for j in range(D):
        req[j // Z, j % Z] = wanted[j:j + 1, :]
    place = blocks * float(cap) + slot
    for k in range(S // 128):
        t = jnp.transpose(jnp.broadcast_to(place[k * 128:(k + 1) * 128, :], (128, 128)))
        own[k] = t[0:1, :].astype(jnp.int32)
    oc = pltpu.make_async_copy(own, owns, l_sem.at[0])
    oc.start()

    for j in xpeers:
        c_rx(j).start()
    reqx[mx] = req[mx]
    sends(c_sec, D // 4, D // 2)
    for j in xpeers:
        w_rx(j).wait_recv()
    for k in range(1, Z):
        c_rz(zpeers(k)).start()
    sends(c_sec, D // 2, D)
    reqr[:, mz] = reqx[:, mz]
    recv[pl.ds(pl.multiple_of(me * rb, rb), rb), :] = v[pl.ds(pl.multiple_of(me * rb, rb), rb), :]
    table[rows:rows + 8, :] = jnp.zeros((8, W), f32)
    for k in range(1, Z):
        w_rz(zpeers(k)).wait_recv()
    rc = pltpu.make_async_copy(reqr, reqs, l_sem.at[1])
    rc.start()
    rc.wait()
    oc.wait()
    all_sec.wait_recv()

    lowb = rb.bit_length() - 1
    left, low, first = D.bit_length() - 1, lowb, True
    while left:
        b = min(3, left)
        left -= b
        mix_pass(recv if first else table, table, rows, low, b, norm if left == 0 else None)
        low, first = low + b, False

    R = D * cap
    for x in range(X):
        def answer(z, _, x=x):
            for c in range(cap):
                ans[x, pl.ds(z * cap + c, 1), :] = table[pl.ds(jnp.clip(reqs[x, z, 0, c], 0, rows), 1), :]
            return 0
        lax.fori_loop(0, Z, answer, 0, unroll=2 if Z % 2 == 0 else 1)
        xall[col, x * Z * cap:(x + 1) * Z * cap, :] = ans[x]

    half = R // 2
    up, down = lax.rem(col + 2, C), lax.rem(col + C - 2, C)

    def c_col(s, h, t):
        ref = xall.at[s, pl.ds(h * half, half), :]
        return rcopy(ref, ref, s_col.at[s, h, t], r_col.at[s, h], c=(sib, up, down)[t])
    started = []

    def go(s, h, t):
        started.append(c_col(s, h, t))
        started[-1].start()
    ring = C > 4
    far = lax.rem(col + 4, C)
    go(col, 0, 2)
    go(col, 1, 1 if ring else 2)
    go(col, 0, 0)
    go(col, 1, 0)
    if ring:
        go(col, 1, 2)
        go(col, 0, 1)
    slots = lambda ref, z: ref.at[:, pl.ds(pl.multiple_of(z * cap, 8), cap), :]
    c_az = lambda j: rcopy(slots(ans, j), slots(ansz, mz), s_az.at[j], r_az.at[mz], row=mx * Z + j)
    w_az = lambda j: rcopy(slots(ans, j), slots(ansz, j), s_az.at[j], r_az.at[j], row=mx * Z + j)
    flat = lambda x: ret.at[pl.ds(pl.multiple_of(x * Z * cap, 8), Z * cap), :]
    c_ax = lambda j: rcopy(ansz.at[j], flat(mx), s_ax.at[j], r_ax.at[mx], row=j * Z + mz)
    w_ax = lambda j: rcopy(ansz.at[j], flat(j), s_ax.at[j], r_ax.at[j], row=j * Z + mz)

    mine = jnp.transpose(xall[col])

    def block(s):
        part[pl.ds(pl.multiple_of(s * W, W), W), :] = jnp.transpose(
            jnp.dot(mine, xall[s], precision=HI, preferred_element_type=f32))
    q = C * W // X
    xs = lambda j: part.at[pl.ds(pl.multiple_of(j * q, q), q), :]
    c_x = lambda j: rcopy(xs(j), xr.at[mx], s_x.at[j], r_x.at[mx], row=j * Z + mz)
    w_x = lambda j: rcopy(xs(j), xr.at[j], s_x.at[j], r_x.at[j], row=j * Z + mz)
    per_x = X * 2 // C
    chip = col // 2

    def along(k):
        a, b = lax.rem(col + 2 * k, C), lax.rem(sib + 2 * k, C)
        for h in range(2):
            c_col(b, h, 0).wait_recv()
        block(a)
        block(b)
        j = lax.rem(chip + k, C // 2)
        for n in range(per_x):
            @pl.when(mx != j * per_x + n)
            def _():
                c_x(j * per_x + n).start()
    if ring:
        along(0)
        c_col(up, 0, 0).wait_recv()
        go(up, 0, 2)
        go(up, 0, 0)
        c_col(down, 1, 0).wait_recv()
        go(down, 1, 1)
        go(down, 1, 0)
        c_col(up, 1, 0).wait_recv()
        go(up, 1, 0)
        c_col(down, 0, 0).wait_recv()
        go(down, 0, 0)
        along(1)
        along(3)
        for h in range(2):
            c_col(far, h, 0).wait_recv()
            go(far, h, 0)
        along(2)
    else:
        for h in range(2):
            c_col(up, h, 0).wait_recv()
            go(up, h, 0)
        along(0)
        along(1)

    xr[mx] = part[pl.ds(pl.multiple_of(mx * q, q), q), :]

    for j in xpeers:
        w_x(j).wait_recv()
    acc = xr[0]
    for j in range(1, X):
        acc = acc + xr[j]
    e = q // Z
    zs[...] = acc.reshape(Z, e, W)
    c_z = lambda j: rcopy(zs.at[j], zr.at[mz], s_z.at[j], r_z.at[mz], row=mx * Z + j)
    w_z = lambda j: rcopy(zs.at[j], zr.at[j], s_z.at[j], r_z.at[j], row=mx * Z + j)
    for k in range(1, Z):
        c_z(zpeers(k)).start()
    zr[mz] = zs[mz]
    for k in range(1, Z):
        w_z(zpeers(k)).wait_recv()
    acc = zr[0]
    for j in range(1, Z):
        acc = acc + zr[j]
    gb[col, pl.ds(pl.multiple_of(mx * q + mz * e, e), e), :] = acc / samples
    ze = lambda j: gb.at[col, pl.ds(pl.multiple_of(mx * q + j * e, e), e), :]
    c_zg = lambda j: rcopy(ze(mz), ze(mz), s_zg.at[j], r_zg.at[mz], row=mx * Z + j)
    w_zg = lambda j: rcopy(ze(j), ze(j), s_zg.at[j], r_zg.at[j], row=mx * Z + j)
    for k in range(1, Z):
        c_zg(zpeers(k)).start()
    for k in range(1, Z):
        c_az(zpeers(k)).start()
    ansz[:, pl.ds(pl.multiple_of(mz * cap, 8), cap), :] = ans[:, pl.ds(pl.multiple_of(mz * cap, 8), cap), :]
    for k in range(1, Z):
        w_zg(zpeers(k)).wait_recv()
    per = C // X
    gblk = lambda s, p: gb.at[s, pl.ds(pl.multiple_of(p * W, W), W), :]
    c_xg = lambda p, j: rcopy(gblk(col, p), gblk(col, p), s_xg.at[p, j], r_xg.at[p], row=j * Z + mz)
    c_cg = lambda p, k: rcopy(gblk(col, p), gblk(col, p), s_cg.at[p, k], r_cg.at[col, p], c=ypeers[k])
    c_fw = lambda s, p: rcopy(gblk(s, p), gblk(s, p), s_fw.at[s, p], r_cg.at[s, p], c=sib)

    def along_x(p):
        @pl.when((mx == p // per) & (p <= col))
        def _():
            for j in xpeers:
                c_xg(p, j).start()

    def own_block(p):
        @pl.when(p <= col)
        def _():
            @pl.when(mx != p // per)
            def _():
                c_xg(p, mx).wait_recv()
            c_fw(col, p).start()
            for k in (1, 0, 2) if len(ypeers) == 3 else range(len(ypeers)):
                c_cg(p, k).start()

    def pass_on(p):
        for s in ypeers:
            @pl.when(p <= s)
            def _():
                c_fw(s, p).wait_recv()
                c_fw(s, p).start()

    def arrived(p):
        for k in range(C // 2):
            s = lax.rem(sib + 2 * k, C)

            @pl.when(p <= s)
            def _():
                c_fw(s, p).wait_recv()

    def each(fn, lo, hi):
        lax.fori_loop(lo, hi, lambda p, _: (fn(p), 0)[1], 0)
    each(along_x, 0, C)
    own_block(0)
    own_block(1)
    u[...] = jnp.zeros_like(u)
    own_block(2)
    pass_on(0)

    pr = lax.broadcasted_iota(jnp.int32, (W, W), 0)
    pc = lax.broadcasted_iota(jnp.int32, (W, W), 1)

    def panel(p, _):
        for ahead, fn in ((3, own_block), (1, pass_on)):
            @pl.when(p + ahead < C)
            def _():
                fn(p + ahead)
        arrived(p)
        base = pl.multiple_of(p * W, W)
        for pp in range(C):
            @pl.when(p == pp)
            def _():
                a0 = pp * W
                for t in range(pp, C):
                    u[a0:a0 + W, t * W:(t + 1) * W] = gb[t, a0:a0 + W, :]
                if pp:
                    u[a0:a0 + W, a0:] = u[a0:a0 + W, a0:] - lax.dot_general(
                        u[0:a0, a0:a0 + W], u[0:a0, a0:], TN, precision=HI, preferred_element_type=f32)
        aug[:, 0:W] = u[pl.ds(base, W), pl.ds(base, W)]
        aug[:, W:] = jnp.where(pr == pc, 1.0, 0.0).astype(f32)
        panel_factor(aug, upan)
        u[pl.ds(base, W), pl.ds(base, W)] = jnp.where(pr <= pc, upan[:, 0:W], 0.0)
        for pp in range(C - 1):
            @pl.when(p == pp)
            def _():
                a0, a1 = pp * W, (pp + 1) * W
                linv = jnp.where(pr >= pc, upan[:, W:], 0.0)
                u[a0:a1, a1:] = jnp.dot(linv, u[a0:a1, a1:], precision=HI, preferred_element_type=f32)

        @pl.when(p == C // 2)
        def _():
            for k in range(1, Z):
                w_az(zpeers(k)).wait_recv()
            for j in xpeers:
                c_ax(j).start()
            ret[pl.ds(pl.multiple_of(mx * Z * cap, 8), Z * cap), :] = ansz[mx]

        @pl.when(p == C - 2)
        def _():
            for j in xpeers:
                w_ax(j).wait_recv()

            def keep(t, _):
                k, first = t // 16, t % 16
                for i in range(8):
                    at = jnp.clip(owns[k, 0, first * 8 + i], 0, R - 1)
                    sk_ref[pl.ds(t * 8 + i, 1), :] = ret[pl.ds(at, 1), :]
                return 0
            lax.fori_loop(0, S // 8, keep, 0)
        return 0

    lax.fori_loop(0, C, panel, 0)
    here = pl.ds(pl.multiple_of(col * W, W), W)
    for j in range(C):
        fac_ref[j * W:(j + 1) * W, :] = jnp.transpose(u[here, j * W:(j + 1) * W])

    all_sec.wait_send()
    for j in xpeers:
        w_rx(j).wait_send()
        w_ax(j).wait_send()
    for k in range(1, Z):
        w_rz(zpeers(k)).wait_send()
        w_az(zpeers(k)).wait_send()
    for c in started:
        c.wait_send()
    for j in xpeers:
        w_x(j).wait_send()

    def left(p):
        @pl.when(p <= col)
        def _():
            @pl.when(mx == p // per)
            def _():
                for j in xpeers:
                    c_xg(p, j).wait_send()
            for k in range(len(ypeers)):
                c_cg(p, k).wait_send()
            c_fw(col, p).wait_send()
        for s in ypeers:
            @pl.when(p <= s)
            def _():
                c_fw(s, p).wait_send()
    each(left, 0, C)
    for k in range(1, Z):
        w_z(zpeers(k)).wait_send()
        w_zg(zpeers(k)).wait_send()


def exchange(a, signs, blocks, offs, X, Z, C):
    rows, W = a.shape
    D = X * Z
    S = offs.shape[0]
    cap = max(2, 2 * S // D)
    rb = rows // D
    R = D * cap
    q = C * W // X
    V = pltpu.VMEM
    dma = pltpu.SemaphoreType.DMA
    return pl.pallas_call(
        functools.partial(exchange_kernel, X, Z, C, 1.0 / math.sqrt(D * rows), float(D * S)),
        out_shape=(jax.ShapeDtypeStruct((C * W, W), f32), jax.ShapeDtypeStruct((S, W), f32)),
        in_specs=[pl.BlockSpec(memory_space=pl.ANY)] * 4,
        out_specs=(pl.BlockSpec(memory_space=V), pl.BlockSpec(memory_space=V)),
        scratch_shapes=[
            V((rows, W), f32), V((rows // 128, 128), jnp.int32), V((2, S // 128, 128), jnp.int32),
            V((rows, W), f32), V((rows + 8, W), f32),
            V((X, Z, 1, 128), jnp.int32), V((X, Z, 1, 128), jnp.int32), V((X, Z, 1, 128), jnp.int32),
            pltpu.SMEM((X, Z, 1, 128), jnp.int32),
            V((S // 128, 1, 128), jnp.int32), pltpu.SMEM((S // 128, 1, 128), jnp.int32),
            V((X, Z * cap, W), f32), V((X, Z * cap, W), f32), V((R, W), f32), V((C, R, W), f32),
            V((C * W, W), f32), V((X, q, W), f32), V((Z, q // Z, W), f32), V((Z, q // Z, W), f32),
            V((C, C * W, W), f32), V((C * W, C * W), f32), V((W, 2 * W), f32), V((W, 2 * W), f32),
            dma((X,)), dma((X,)), dma((Z,)), dma((Z,)), dma((1,)), dma((1,)), dma((Z,)), dma((Z,)), dma((X,)), dma((X,)),
            dma((C, 2, 3)), dma((C, 2)), dma((X,)), dma((X,)), dma((Z,)), dma((Z,)),
            dma((Z,)), dma((Z,)), dma((C, X)), dma((C,)), dma((C, C // 2)), dma((C, C)), dma((C, C)), dma((6,)),
        ],
        compiler_params=pltpu.CompilerParams(collective_id=0, has_side_effects=True, vmem_limit_bytes=60 * 2**20),
        name="exchange",
    )(a, signs.reshape(rows // 128, 128), blocks.reshape(S // 128, 128), offs.reshape(S // 128, 128))


def solution(mesh):
    x_size, z_size, c_size = 4, mesh.shape["row"] // 4, mesh.shape["col"]

    def shards(matrix, row_signs, sample_block, sample_offset):
        factor, sketch = exchange(matrix, row_signs, sample_block, sample_offset, x_size, z_size, c_size)
        return sketch, factor

    placed = (P("row", "col"), P("row"), P("row", None), P("row"))
    return jax.shard_map(
        shards,
        mesh=mesh,
        in_specs=placed,
        out_specs=(P("row", "col"), P(None, "col")),
        check_vma=False,
    )
```

```python
import functools
import math

import jax
import jax.numpy as jnp
from jax import lax
from jax.experimental import pallas as pl
from jax.experimental.pallas import tpu as pltpu
from jax.sharding import PartitionSpec as P

f32, bf16 = jnp.float32, jnp.bfloat16
TN = (((0,), (0,)), ((), ()))
HI = lax.Precision.HIGHEST


def butterflies(v):
    n, step = len(v), 1
    while step < n:
        v = [v[i] + v[i + step] if not i & step else v[i - step] - v[i] for i in range(n)]
        step *= 2
    return v


def mix_pass(src, dst, rows, low, bits, scale=None):
    n, stride = 1 << bits, 1 << low
    tiles = stride // 8
    groups = rows // (n * stride)

    def body(t, _):
        g, j = t // tiles, t % tiles
        base = g * (n * stride) + j * 8
        v = [src[pl.ds(pl.multiple_of(base + i * stride, 8), 8), :] for i in range(n)]
        v = butterflies(v)
        for i in range(n):
            dst[pl.ds(pl.multiple_of(base + i * stride, 8), 8), :] = v[i] if scale is None else v[i] * scale
        return 0

    lax.fori_loop(0, groups * tiles, body, 0, unroll=2 if groups * tiles % 2 == 0 else 1)


PAN = 128
BLK = 16


def panel_factor(aug, upan):
    wide = 2 * PAN
    lanes = wide // PAN
    cur = [[aug[8 * r:8 * r + 8, h * PAN:(h + 1) * PAN] for h in range(lanes)] for r in range(BLK // 8)]
    nblk, sub = PAN // BLK, BLK // 8
    for t in range(nblk):
        lo = t * BLK
        last = t == nblk - 1
        C = [[jnp.broadcast_to(cur[r][0][:, lo + k:lo + k + 1], (8, PAN)) for r in range(sub)] for k in range(BLK)]
        if not last:
            xt = jnp.transpose(jnp.concatenate([cur[r][0] for r in range(sub)], axis=0))[lo + BLK:lo + 2 * BLK, :]
            N = [[jnp.broadcast_to(xt[8 * r:8 * r + 8, k:k + 1], (8, PAN)) for r in range(sub)] for k in range(BLK)]
            nxt = aug[lo + BLK:lo + 2 * BLK, :]
            if t > 0:
                done = upan[0:lo, :]
                nxt = nxt - lax.dot_general(done[:, lo + BLK:lo + 2 * BLK], done, TN,
                                            precision=HI, preferred_element_type=f32)
            acc = [[None] * lanes for _ in range(sub)]
        R = cur
        for k in range(BLK):
            rs = lax.rsqrt(C[k][k // 8][k % 8:k % 8 + 1, :])
            u = [R[k // 8][h][k % 8:k % 8 + 1, :] * rs for h in range(lanes)]
            for h in range(lanes):
                upan[lo + k:lo + k + 1, h * PAN:(h + 1) * PAN] = u[h]
            first = (k + 1) // 8
            L = [C[k][r] * rs if r >= first else None for r in range(sub)]
            Nl = [N[k][r] * rs for r in range(sub)] if not last else None
            for c in range(k + 1, BLK):
                m = L[c // 8][c % 8:c % 8 + 1, :]
                for r in range(c // 8, sub):
                    C[c][r] = C[c][r] - L[r] * m
                if not last:
                    for r in range(sub):
                        N[c][r] = N[c][r] - Nl[r] * m
            for h in range(lanes):
                for r in range(first, sub):
                    R[r][h] = R[r][h] - L[r] * u[h]
                if not last:
                    for r in range(sub):
                        acc[r][h] = Nl[r] * u[h] if acc[r][h] is None else acc[r][h] + Nl[r] * u[h]
        if not last:
            cur = [[nxt[8 * r:8 * r + 8, h * PAN:(h + 1) * PAN] - acc[r][h] for h in range(lanes)] for r in range(sub)]


def split2(x):
    h = x.astype(bf16)
    return h, (x - h.astype(f32)).astype(bf16)


def dot3(a, b):
    ah, al = split2(a)
    bh, bl = split2(b)
    return jnp.dot(jnp.concatenate([ah, al], axis=1), jnp.concatenate([bh, bh], axis=0), preferred_element_type=f32) \
        + jnp.dot(ah, bl, preferred_element_type=f32)


def exchange_kernel(X, Z, C, norm, samples,
                    a_ref, sign_ref, blk_ref, off_ref,
                    fac_ref, sk_ref,
                    v, sign, pos, recv, table, req, reqx, reqr, reqs, own, owns, ans, ansz, ret, xall, part, xr, zs, zr,
                    gb, u, aug, upan,
                    s_rx, r_rx, s_rz, r_rz, s_sec, r_sec, s_az, r_az, s_ax, r_ax, s_col, r_col, s_x, r_x, s_z, r_z,
                    s_zg, r_zg, s_xg, r_xg, s_cg, s_fw, r_cg, l_sem):
    D = X * Z
    rows, W = v.shape
    rb = rows // D
    cap = ret.shape[0] // D
    SR = blk_ref.shape[0]
    S = SR * 128
    me, col = lax.axis_index("row"), lax.axis_index("col")
    mx, mz = me // Z, me % Z
    sib = col + 1 - 2 * (col % 2)

    def rcopy(src, dst, ss, rs, row=None, c=None):
        dev = {"row": row} if c is None else {"col": c}
        return pltpu.make_async_remote_copy(src_ref=src, dst_ref=dst, send_sem=ss, recv_sem=rs,
                                            device_id=dev, device_id_type=pl.DeviceIdType.MESH)

    bar = pltpu.get_barrier_semaphore()

    def greet(k, _):
        pl.semaphore_signal(bar, inc=1, device_id={"row": lax.rem(me + k, D)}, device_id_type=pl.DeviceIdType.MESH)
        return 0
    lax.fori_loop(1, D, greet, 0)
    ypeers = [lax.rem(col + 2 * k, C) for k in range(1, C // 2)]
    for c in [sib] + ypeers:
        pl.semaphore_signal(bar, inc=1, device_id={"col": c}, device_id_type=pl.DeviceIdType.MESH)

    fetch = [pltpu.make_async_copy(src, dst, l_sem.at[2 + k]) for k, (src, dst) in enumerate(
        [(blk_ref, pos.at[0]), (off_ref, pos.at[1]), (sign_ref, sign), (a_ref, v)])]
    for c in fetch:
        c.start()
    nb = rows // 128
    fetch[2].wait()
    fetch[3].wait()
    st = jnp.transpose(jnp.concatenate([sign[...].astype(f32), jnp.zeros((128 - nb, 128), f32)], axis=0))
    for j in range(nb):
        v[j * 128:(j + 1) * 128, :] = v[j * 128:(j + 1) * 128, :] * jnp.broadcast_to(st[:, j:j + 1], (128, W))

    def low_bits(g, _):
        base = pl.multiple_of(g * 64, 64)
        w = butterflies([v[pl.ds(base + k, 8, stride=8), :] for k in range(8)])
        for k in range(8):
            v[pl.ds(base + k, 8, stride=8), :] = w[k]
        return 0
    lax.fori_loop(0, rows // 64, low_bits, 0, unroll=2)
    left, low = rows.bit_length() - 1 - 3, 3
    while left:
        b = min(3, left)
        mix_pass(v, v, rows, low, b)
        low, left = low + b, left - b

    pl.semaphore_wait(bar, D - 1 + 1 + len(ypeers))

    def peer_of(k):
        return lax.rem(me + jnp.where(k % 2 == 1, (k + 1) // 2, D - k // 2), D)

    def sends(fn, lo, hi):
        def go(k, _):
            fn(peer_of(k)).start()
            return 0
        lax.fori_loop(lo, hi, go, 0)

    xpeers = [lax.rem(mx + k, X) for k in range(1, X)]
    zpeers = lambda k: lax.rem(mz + k, Z)
    c_rx = lambda j: rcopy(req.at[j], reqx.at[mx], s_rx.at[j], r_rx.at[mx], row=j * Z + mz)
    w_rx = lambda j: rcopy(req.at[j], reqx.at[j], s_rx.at[j], r_rx.at[j], row=j * Z + mz)
    c_rz = lambda j: rcopy(reqx.at[:, j], reqr.at[:, mz], s_rz.at[j], r_rz.at[mz], row=mx * Z + j)
    w_rz = lambda j: rcopy(reqx.at[:, j], reqr.at[:, j], s_rz.at[j], r_rz.at[j], row=mx * Z + j)
    sec = lambda j: v.at[pl.ds(pl.multiple_of(j * rb, rb), rb), :]
    got = lambda j: recv.at[pl.ds(pl.multiple_of(j * rb, rb), rb), :]
    c_sec = lambda j: rcopy(sec(j), got(me), s_sec.at[0], r_sec.at[0], row=j)
    others = pl.ds(0, (D - 1) * rb)
    all_sec = rcopy(v.at[others, :], recv.at[others, :], s_sec.at[0], r_sec.at[0], row=lax.rem(me + 1, D))
    sends(c_sec, 1, D // 4)
    fetch[0].wait()
    fetch[1].wait()

    both = jnp.transpose(jnp.concatenate(
        [pos[0].astype(f32), pos[1].astype(f32), jnp.zeros((128 - 2 * SR, 128), f32)], axis=0))
    blocks, offc = [jnp.concatenate([both[:, k:k + 1] for k in range(b, b + SR)], axis=0) for b in (0, SR)]
    lane = lax.broadcasted_iota(jnp.int32, (S, 128), 1)
    onehot = (blocks == lane.astype(f32)).astype(f32)
    ri = lax.broadcasted_iota(jnp.int32, (S, S), 0)
    ci = lax.broadcasted_iota(jnp.int32, (S, S), 1)
    before = jnp.dot((ci < ri).astype(bf16), onehot.astype(bf16), preferred_element_type=f32)
    slot = jnp.sum(before * onehot, axis=1, keepdims=True)
    val = jnp.where(lane.astype(f32) == slot, offc - float(rows), 0.0)
    wanted = lax.dot_general(onehot, val, TN, precision=HI, preferred_element_type=f32) + float(rows)
    wanted = wanted.astype(jnp.int32)
    for j in range(D):
        req[j // Z, j % Z] = wanted[j:j + 1, :]
    place = blocks * float(cap) + slot
    for k in range(S // 128):
        t = jnp.transpose(jnp.broadcast_to(place[k * 128:(k + 1) * 128, :], (128, 128)))
        own[k] = t[0:1, :].astype(jnp.int32)
    oc = pltpu.make_async_copy(own, owns, l_sem.at[0])
    oc.start()

    for j in xpeers:
        c_rx(j).start()
    reqx[mx] = req[mx]
    sends(c_sec, D // 4, D // 2)
    for j in xpeers:
        w_rx(j).wait_recv()
    for k in range(1, Z):
        c_rz(zpeers(k)).start()
    sends(c_sec, D // 2, D)
    reqr[:, mz] = reqx[:, mz]
    recv[pl.ds(pl.multiple_of(me * rb, rb), rb), :] = v[pl.ds(pl.multiple_of(me * rb, rb), rb), :]
    table[rows:rows + 8, :] = jnp.zeros((8, W), f32)
    for k in range(1, Z):
        w_rz(zpeers(k)).wait_recv()
    rc = pltpu.make_async_copy(reqr, reqs, l_sem.at[1])
    rc.start()
    rc.wait()
    oc.wait()
    all_sec.wait_recv()

    lowb = rb.bit_length() - 1
    left, low, first = D.bit_length() - 1, lowb, True
    while left:
        b = min(3, left)
        left -= b
        mix_pass(recv if first else table, table, rows, low, b, norm if left == 0 else None)
        low, first = low + b, False

    R = D * cap
    for x in range(X):
        def answer(z, _, x=x):
            for c in range(cap):
                ans[x, pl.ds(z * cap + c, 1), :] = table[pl.ds(jnp.clip(reqs[x, z, 0, c], 0, rows), 1), :]
            return 0
        lax.fori_loop(0, Z, answer, 0, unroll=2 if Z % 2 == 0 else 1)
        xall[col, x * Z * cap:(x + 1) * Z * cap, :] = ans[x]

    half = R // 2
    up, down = lax.rem(col + 2, C), lax.rem(col + C - 2, C)

    def c_col(s, h, t):
        ref = xall.at[s, pl.ds(h * half, half), :]
        return rcopy(ref, ref, s_col.at[s, h, t], r_col.at[s, h], c=(sib, up, down)[t])
    started = []

    def go(s, h, t):
        started.append(c_col(s, h, t))
        started[-1].start()
    ring = C > 4
    far = lax.rem(col + 4, C)
    go(col, 0, 2)
    go(col, 1, 1 if ring else 2)
    go(col, 0, 0)
    go(col, 1, 0)
    if ring:
        go(col, 1, 2)
        go(col, 0, 1)
    slots = lambda ref, z: ref.at[:, pl.ds(pl.multiple_of(z * cap, 8), cap), :]
    c_az = lambda j: rcopy(slots(ans, j), slots(ansz, mz), s_az.at[j], r_az.at[mz], row=mx * Z + j)
    w_az = lambda j: rcopy(slots(ans, j), slots(ansz, j), s_az.at[j], r_az.at[j], row=mx * Z + j)
    flat = lambda x: ret.at[pl.ds(pl.multiple_of(x * Z * cap, 8), Z * cap), :]
    c_ax = lambda j: rcopy(ansz.at[j], flat(mx), s_ax.at[j], r_ax.at[mx], row=j * Z + mz)
    w_ax = lambda j: rcopy(ansz.at[j], flat(j), s_ax.at[j], r_ax.at[j], row=j * Z + mz)
    for k in range(1, Z):
        c_az(zpeers(k)).start()
    ansz[:, pl.ds(pl.multiple_of(mz * cap, 8), cap), :] = ans[:, pl.ds(pl.multiple_of(mz * cap, 8), cap), :]

    mine = jnp.transpose(xall[col])

    def block(s):
        part[pl.ds(pl.multiple_of(s * W, W), W), :] = jnp.transpose(
            jnp.dot(mine, xall[s], precision=HI, preferred_element_type=f32))
    q = C * W // X
    xs = lambda j: part.at[pl.ds(pl.multiple_of(j * q, q), q), :]
    c_x = lambda j: rcopy(xs(j), xr.at[mx], s_x.at[j], r_x.at[mx], row=j * Z + mz)
    w_x = lambda j: rcopy(xs(j), xr.at[j], s_x.at[j], r_x.at[j], row=j * Z + mz)
    per_x = X * 2 // C
    chip = col // 2

    def along(k):
        a, b = lax.rem(col + 2 * k, C), lax.rem(sib + 2 * k, C)
        for h in range(2):
            c_col(b, h, 0).wait_recv()
        block(a)
        block(b)
        j = lax.rem(chip + k, C // 2)
        for n in range(per_x):
            @pl.when(mx != j * per_x + n)
            def _():
                c_x(j * per_x + n).start()
    if ring:
        along(0)
        c_col(up, 0, 0).wait_recv()
        go(up, 0, 2)
        go(up, 0, 0)
        c_col(down, 1, 0).wait_recv()
        go(down, 1, 1)
        go(down, 1, 0)
        c_col(up, 1, 0).wait_recv()
        go(up, 1, 0)
        c_col(down, 0, 0).wait_recv()
        go(down, 0, 0)
        along(1)
        along(3)
        for h in range(2):
            c_col(far, h, 0).wait_recv()
            go(far, h, 0)
        along(2)
    else:
        for h in range(2):
            c_col(up, h, 0).wait_recv()
            go(up, h, 0)
        along(0)
        along(1)

    xr[mx] = part[pl.ds(pl.multiple_of(mx * q, q), q), :]

    for j in xpeers:
        w_x(j).wait_recv()
    acc = xr[0]
    for j in range(1, X):
        acc = acc + xr[j]
    e = q // Z
    zs[...] = acc.reshape(Z, e, W)
    c_z = lambda j: rcopy(zs.at[j], zr.at[mz], s_z.at[j], r_z.at[mz], row=mx * Z + j)
    w_z = lambda j: rcopy(zs.at[j], zr.at[j], s_z.at[j], r_z.at[j], row=mx * Z + j)
    for k in range(1, Z):
        c_z(zpeers(k)).start()
    zr[mz] = zs[mz]
    for k in range(1, Z):
        w_az(zpeers(k)).wait_recv()
    for j in xpeers:
        c_ax(j).start()
    ret[pl.ds(pl.multiple_of(mx * Z * cap, 8), Z * cap), :] = ansz[mx]
    for k in range(1, Z):
        w_z(zpeers(k)).wait_recv()
    acc = zr[0]
    for j in range(1, Z):
        acc = acc + zr[j]
    gb[col, pl.ds(pl.multiple_of(mx * q + mz * e, e), e), :] = acc / samples
    ze = lambda j: gb.at[col, pl.ds(pl.multiple_of(mx * q + j * e, e), e), :]
    c_zg = lambda j: rcopy(ze(mz), ze(mz), s_zg.at[j], r_zg.at[mz], row=mx * Z + j)
    w_zg = lambda j: rcopy(ze(j), ze(j), s_zg.at[j], r_zg.at[j], row=mx * Z + j)
    for k in range(1, Z):
        c_zg(zpeers(k)).start()
    for k in range(1, Z):
        w_zg(zpeers(k)).wait_recv()
    per = C // X
    gblk = lambda s, p: gb.at[s, pl.ds(pl.multiple_of(p * W, W), W), :]
    c_xg = lambda p, j: rcopy(gblk(col, p), gblk(col, p), s_xg.at[p, j], r_xg.at[p], row=j * Z + mz)
    c_cg = lambda p, k: rcopy(gblk(col, p), gblk(col, p), s_cg.at[p, k], r_cg.at[col, p], c=ypeers[k])
    c_fw = lambda s, p: rcopy(gblk(s, p), gblk(s, p), s_fw.at[s, p], r_cg.at[s, p], c=sib)

    def along_x(p):
        @pl.when((mx == p // per) & (p <= col))
        def _():
            for j in xpeers:
                c_xg(p, j).start()

    def own_block(p):
        @pl.when(p <= col)
        def _():
            @pl.when(mx != p // per)
            def _():
                c_xg(p, mx).wait_recv()
            c_fw(col, p).start()
            for k in (1, 0, 2) if len(ypeers) == 3 else range(len(ypeers)):
                c_cg(p, k).start()

    def pass_on(p):
        for s in ypeers:
            @pl.when(p <= s)
            def _():
                c_fw(s, p).wait_recv()
                c_fw(s, p).start()

    def arrived(p):
        for k in range(C // 2):
            s = lax.rem(sib + 2 * k, C)

            @pl.when(p <= s)
            def _():
                c_fw(s, p).wait_recv()

    def each(fn, lo, hi):
        lax.fori_loop(lo, hi, lambda p, _: (fn(p), 0)[1], 0)
    each(along_x, 0, C)
    own_block(0)
    own_block(1)
    u[...] = jnp.zeros_like(u)
    for j in xpeers:
        w_ax(j).wait_recv()

    def keep(t, _):
        k, first = t // 16, t % 16
        for i in range(8):
            at = jnp.clip(owns[k, 0, first * 8 + i], 0, R - 1)
            sk_ref[pl.ds(t * 8 + i, 1), :] = ret[pl.ds(at, 1), :]
        return 0
    lax.fori_loop(0, S // 8, keep, 0)
    pass_on(0)
    own_block(2)
    all_sec.wait_send()
    for j in xpeers:
        w_rx(j).wait_send()
    for k in range(1, Z):
        w_rz(zpeers(k)).wait_send()
        w_az(zpeers(k)).wait_send()
        w_z(zpeers(k)).wait_send()

    pr = lax.broadcasted_iota(jnp.int32, (W, W), 0)
    pc = lax.broadcasted_iota(jnp.int32, (W, W), 1)

    def panel(p, _):
        for ahead, fn in ((3, own_block), (1, pass_on)):
            @pl.when((p > 0) & (p + ahead < C))
            def _():
                fn(p + ahead)
        arrived(p)
        base = pl.multiple_of(p * W, W)
        for pp in range(C):
            @pl.when(p == pp)
            def _():
                a0 = pp * W
                for t in range(pp, C):
                    u[a0:a0 + W, t * W:(t + 1) * W] = gb[t, a0:a0 + W, :]
                if pp:
                    u[a0:a0 + W, a0:] = u[a0:a0 + W, a0:] - dot3(
                        jnp.transpose(u[0:a0, a0:a0 + W]), u[0:a0, a0:])
        aug[:, 0:W] = u[pl.ds(base, W), pl.ds(base, W)]
        aug[:, W:] = jnp.where(pr == pc, 1.0, 0.0).astype(f32)
        panel_factor(aug, upan)
        u[pl.ds(base, W), pl.ds(base, W)] = jnp.where(pr <= pc, upan[:, 0:W], 0.0)

        @pl.when(p == 0)
        def _():
            own_block(3)
            pass_on(1)
        for pp in range(C - 1):
            @pl.when(p == pp)
            def _():
                a0, a1 = pp * W, (pp + 1) * W
                linv = jnp.where(pr >= pc, upan[:, W:], 0.0)
                u[a0:a1, a1:] = dot3(linv, u[a0:a1, a1:])
        return 0

    lax.fori_loop(0, C, panel, 0)
    here = pl.ds(pl.multiple_of(col * W, W), W)
    for j in range(C):
        fac_ref[j * W:(j + 1) * W, :] = jnp.transpose(u[here, j * W:(j + 1) * W])

    for j in xpeers:
        w_ax(j).wait_send()
    for c in started:
        c.wait_send()
    for j in xpeers:
        w_x(j).wait_send()

    def left(p):
        @pl.when(p <= col)
        def _():
            @pl.when(mx == p // per)
            def _():
                for j in xpeers:
                    c_xg(p, j).wait_send()
            for k in range(len(ypeers)):
                c_cg(p, k).wait_send()
            c_fw(col, p).wait_send()
        for s in ypeers:
            @pl.when(p <= s)
            def _():
                c_fw(s, p).wait_send()
    each(left, 0, C)
    for k in range(1, Z):
        w_zg(zpeers(k)).wait_send()


def exchange(a, signs, blocks, offs, X, Z, C):
    rows, W = a.shape
    D = X * Z
    S = offs.shape[0]
    cap = max(2, 2 * S // D)
    rb = rows // D
    R = D * cap
    q = C * W // X
    V = pltpu.VMEM
    dma = pltpu.SemaphoreType.DMA
    return pl.pallas_call(
        functools.partial(exchange_kernel, X, Z, C, 1.0 / math.sqrt(D * rows), float(D * S)),
        out_shape=(jax.ShapeDtypeStruct((C * W, W), f32), jax.ShapeDtypeStruct((S, W), f32)),
        in_specs=[pl.BlockSpec(memory_space=pl.ANY)] * 4,
        out_specs=(pl.BlockSpec(memory_space=V), pl.BlockSpec(memory_space=V)),
        scratch_shapes=[
            V((rows, W), f32), V((rows // 128, 128), jnp.int32), V((2, S // 128, 128), jnp.int32),
            V((rows, W), f32), V((rows + 8, W), f32),
            V((X, Z, 1, 128), jnp.int32), V((X, Z, 1, 128), jnp.int32), V((X, Z, 1, 128), jnp.int32),
            pltpu.SMEM((X, Z, 1, 128), jnp.int32),
            V((S // 128, 1, 128), jnp.int32), pltpu.SMEM((S // 128, 1, 128), jnp.int32),
            V((X, Z * cap, W), f32), V((X, Z * cap, W), f32), V((R, W), f32), V((C, R, W), f32),
            V((C * W, W), f32), V((X, q, W), f32), V((Z, q // Z, W), f32), V((Z, q // Z, W), f32),
            V((C, C * W, W), f32), V((C * W, C * W), f32), V((W, 2 * W), f32), V((W, 2 * W), f32),
            dma((X,)), dma((X,)), dma((Z,)), dma((Z,)), dma((1,)), dma((1,)), dma((Z,)), dma((Z,)), dma((X,)), dma((X,)),
            dma((C, 2, 3)), dma((C, 2)), dma((X,)), dma((X,)), dma((Z,)), dma((Z,)),
            dma((Z,)), dma((Z,)), dma((C, X)), dma((C,)), dma((C, C // 2)), dma((C, C)), dma((C, C)), dma((6,)),
        ],
        compiler_params=pltpu.CompilerParams(collective_id=0, has_side_effects=True, vmem_limit_bytes=60 * 2**20),
        name="exchange",
    )(a, signs.reshape(rows // 128, 128), blocks.reshape(S // 128, 128), offs.reshape(S // 128, 128))


def solution(mesh):
    x_size, z_size, c_size = 4, mesh.shape["row"] // 4, mesh.shape["col"]

    def shards(matrix, row_signs, sample_block, sample_offset):
        factor, sketch = exchange(matrix, row_signs, sample_block, sample_offset, x_size, z_size, c_size)
        return sketch, factor

    placed = (P("row", "col"), P("row"), P("row", None), P("row"))
    return jax.shard_map(
        shards,
        mesh=mesh,
        in_specs=placed,
        out_specs=(P("row", "col"), P(None, "col")),
        check_vma=False,
    )
```

```python
import functools
import math

import jax
import jax.numpy as jnp
from jax import lax
from jax.experimental import pallas as pl
from jax.experimental.pallas import tpu as pltpu
from jax.sharding import PartitionSpec as P

f32, bf16 = jnp.float32, jnp.bfloat16
TN = (((0,), (0,)), ((), ()))
HI = lax.Precision.HIGHEST


def butterflies(v):
    n, step = len(v), 1
    while step < n:
        v = [v[i] + v[i + step] if not i & step else v[i - step] - v[i] for i in range(n)]
        step *= 2
    return v


def mix_pass(src, dst, rows, low, bits, scale=None):
    n, stride = 1 << bits, 1 << low
    tiles = stride // 8
    groups = rows // (n * stride)

    def body(t, _):
        g, j = t // tiles, t % tiles
        base = g * (n * stride) + j * 8
        v = [src[pl.ds(pl.multiple_of(base + i * stride, 8), 8), :] for i in range(n)]
        v = butterflies(v)
        for i in range(n):
            dst[pl.ds(pl.multiple_of(base + i * stride, 8), 8), :] = v[i] if scale is None else v[i] * scale
        return 0

    lax.fori_loop(0, groups * tiles, body, 0, unroll=2 if groups * tiles % 2 == 0 else 1)


PAN = 128
BLK = 16


def panel_factor(aug, upan):
    wide = 2 * PAN
    lanes = wide // PAN
    cur = [[aug[8 * r:8 * r + 8, h * PAN:(h + 1) * PAN] for h in range(lanes)] for r in range(BLK // 8)]
    nblk, sub = PAN // BLK, BLK // 8
    for t in range(nblk):
        lo = t * BLK
        last = t == nblk - 1
        C = [[jnp.broadcast_to(cur[r][0][:, lo + k:lo + k + 1], (8, PAN)) for r in range(sub)] for k in range(BLK)]
        if not last:
            xt = jnp.transpose(jnp.concatenate([cur[r][0] for r in range(sub)], axis=0))[lo + BLK:lo + 2 * BLK, :]
            N = [[jnp.broadcast_to(xt[8 * r:8 * r + 8, k:k + 1], (8, PAN)) for r in range(sub)] for k in range(BLK)]
            nxt = aug[lo + BLK:lo + 2 * BLK, :]
            if t > 0:
                done = upan[0:lo, :]
                nxt = nxt - lax.dot_general(done[:, lo + BLK:lo + 2 * BLK], done, TN,
                                            precision=HI, preferred_element_type=f32)
            acc = [[None] * lanes for _ in range(sub)]
        R = cur
        for k in range(BLK):
            rs = lax.rsqrt(C[k][k // 8][k % 8:k % 8 + 1, :])
            u = [R[k // 8][h][k % 8:k % 8 + 1, :] * rs for h in range(lanes)]
            for h in range(lanes):
                upan[lo + k:lo + k + 1, h * PAN:(h + 1) * PAN] = u[h]
            first = (k + 1) // 8
            L = [C[k][r] * rs if r >= first else None for r in range(sub)]
            Nl = [N[k][r] * rs for r in range(sub)] if not last else None
            for c in range(k + 1, BLK):
                m = L[c // 8][c % 8:c % 8 + 1, :]
                for r in range(c // 8, sub):
                    C[c][r] = C[c][r] - L[r] * m
                if not last:
                    for r in range(sub):
                        N[c][r] = N[c][r] - Nl[r] * m
            for h in range(lanes):
                for r in range(first, sub):
                    R[r][h] = R[r][h] - L[r] * u[h]
                if not last:
                    for r in range(sub):
                        acc[r][h] = Nl[r] * u[h] if acc[r][h] is None else acc[r][h] + Nl[r] * u[h]
        if not last:
            cur = [[nxt[8 * r:8 * r + 8, h * PAN:(h + 1) * PAN] - acc[r][h] for h in range(lanes)] for r in range(sub)]


def split2(x):
    h = x.astype(bf16)
    return h, (x - h.astype(f32)).astype(bf16)


def dot3(a, b):
    ah, al = split2(a)
    bh, bl = split2(b)
    return jnp.dot(jnp.concatenate([ah, al], axis=1), jnp.concatenate([bh, bh], axis=0), preferred_element_type=f32) \
        + jnp.dot(ah, bl, preferred_element_type=f32)


def exchange_kernel(X, Z, C, norm, samples,
                    a_ref, sign_ref, blk_ref, off_ref,
                    fac_ref, sk_ref,
                    v, sign, pos, recv, table, req, reqx, reqr, reqs, own, owns, ans, ansz, ret, xall, part, xr, zs, zr,
                    gb, u, aug, upan,
                    s_rx, r_rx, s_rz, r_rz, s_sec, r_sec, s_az, r_az, s_ax, r_ax, s_col, r_col, s_x, r_x, s_z, r_z,
                    s_zg, r_zg, s_xg, r_xg, s_cg, s_fw, r_cg, l_sem):
    D = X * Z
    rows, W = v.shape
    rb = rows // D
    cap = ret.shape[0] // D
    SR = blk_ref.shape[0]
    S = SR * 128
    me, col = lax.axis_index("row"), lax.axis_index("col")
    mx, mz = me // Z, me % Z
    sib = col + 1 - 2 * (col % 2)

    def rcopy(src, dst, ss, rs, row=None, c=None):
        dev = {"row": row} if c is None else {"col": c}
        return pltpu.make_async_remote_copy(src_ref=src, dst_ref=dst, send_sem=ss, recv_sem=rs,
                                            device_id=dev, device_id_type=pl.DeviceIdType.MESH)

    bar = pltpu.get_barrier_semaphore()

    def greet(k, _):
        pl.semaphore_signal(bar, inc=1, device_id={"row": lax.rem(me + k, D)}, device_id_type=pl.DeviceIdType.MESH)
        return 0
    lax.fori_loop(1, D, greet, 0)
    ypeers = [lax.rem(col + 2 * k, C) for k in range(1, C // 2)]
    for c in [sib] + ypeers:
        pl.semaphore_signal(bar, inc=1, device_id={"col": c}, device_id_type=pl.DeviceIdType.MESH)

    fetch = [pltpu.make_async_copy(src, dst, l_sem.at[2 + k]) for k, (src, dst) in enumerate(
        [(blk_ref, pos.at[0]), (off_ref, pos.at[1]), (sign_ref, sign), (a_ref, v)])]
    for c in fetch:
        c.start()
    nb = rows // 128
    fetch[2].wait()
    fetch[3].wait()
    st = jnp.transpose(jnp.concatenate([sign[...].astype(f32), jnp.zeros((128 - nb, 128), f32)], axis=0))
    for j in range(nb):
        v[j * 128:(j + 1) * 128, :] = v[j * 128:(j + 1) * 128, :] * jnp.broadcast_to(st[:, j:j + 1], (128, W))

    def low_bits(g, _):
        base = pl.multiple_of(g * 64, 64)
        w = butterflies([v[pl.ds(base + k, 8, stride=8), :] for k in range(8)])
        for k in range(8):
            v[pl.ds(base + k, 8, stride=8), :] = w[k]
        return 0
    lax.fori_loop(0, rows // 64, low_bits, 0, unroll=2)
    left, low = rows.bit_length() - 1 - 3, 3
    while left:
        b = left if left <= 5 else 3
        mix_pass(v, v, rows, low, b)
        low, left = low + b, left - b

    pl.semaphore_wait(bar, D - 1 + 1 + len(ypeers))

    def peer_of(k):
        return lax.rem(me + jnp.where(k % 2 == 1, (k + 1) // 2, D - k // 2), D)

    def sends(fn, lo, hi):
        def go(k, _):
            fn(peer_of(k)).start()
            return 0
        lax.fori_loop(lo, hi, go, 0)

    xpeers = [lax.rem(mx + k, X) for k in range(1, X)]
    zpeers = lambda k: lax.rem(mz + k, Z)
    c_rx = lambda j: rcopy(req.at[j], reqx.at[mx], s_rx.at[j], r_rx.at[mx], row=j * Z + mz)
    w_rx = lambda j: rcopy(req.at[j], reqx.at[j], s_rx.at[j], r_rx.at[j], row=j * Z + mz)
    c_rz = lambda j: rcopy(reqx.at[:, j], reqr.at[:, mz], s_rz.at[j], r_rz.at[mz], row=mx * Z + j)
    w_rz = lambda j: rcopy(reqx.at[:, j], reqr.at[:, j], s_rz.at[j], r_rz.at[j], row=mx * Z + j)
    sec = lambda j: v.at[pl.ds(pl.multiple_of(j * rb, rb), rb), :]
    got = lambda j: recv.at[pl.ds(pl.multiple_of(j * rb, rb), rb), :]
    c_sec = lambda j: rcopy(sec(j), got(me), s_sec.at[0], r_sec.at[0], row=j)
    others = pl.ds(0, (D - 1) * rb)
    all_sec = rcopy(v.at[others, :], recv.at[others, :], s_sec.at[0], r_sec.at[0], row=lax.rem(me + 1, D))
    sends(c_sec, 1, D // 4)
    fetch[0].wait()
    fetch[1].wait()

    both = jnp.transpose(jnp.concatenate(
        [pos[0].astype(f32), pos[1].astype(f32), jnp.zeros((128 - 2 * SR, 128), f32)], axis=0))
    blocks, offc = [jnp.concatenate([both[:, k:k + 1] for k in range(b, b + SR)], axis=0) for b in (0, SR)]
    lane = lax.broadcasted_iota(jnp.int32, (S, 128), 1)
    onehot = (blocks == lane.astype(f32)).astype(f32)
    ri = lax.broadcasted_iota(jnp.int32, (S, S), 0)
    ci = lax.broadcasted_iota(jnp.int32, (S, S), 1)
    before = jnp.dot((ci < ri).astype(bf16), onehot.astype(bf16), preferred_element_type=f32)
    slot = jnp.sum(before * onehot, axis=1, keepdims=True)
    val = jnp.where(lane.astype(f32) == slot, offc - float(rows), 0.0)
    wanted = lax.dot_general(onehot, val, TN, precision=HI, preferred_element_type=f32) + float(rows)
    wanted = wanted.astype(jnp.int32)
    for j in range(D):
        req[j // Z, j % Z] = wanted[j:j + 1, :]
    place = blocks * float(cap) + slot
    for k in range(S // 128):
        t = jnp.transpose(jnp.broadcast_to(place[k * 128:(k + 1) * 128, :], (128, 128)))
        own[k] = t[0:1, :].astype(jnp.int32)
    oc = pltpu.make_async_copy(own, owns, l_sem.at[0])
    oc.start()

    for j in xpeers:
        c_rx(j).start()
    reqx[mx] = req[mx]
    sends(c_sec, D // 4, D // 2)
    for j in xpeers:
        w_rx(j).wait_recv()
    for k in range(1, Z):
        c_rz(zpeers(k)).start()
    sends(c_sec, D // 2, D)
    reqr[:, mz] = reqx[:, mz]
    recv[pl.ds(pl.multiple_of(me * rb, rb), rb), :] = v[pl.ds(pl.multiple_of(me * rb, rb), rb), :]
    table[rows:rows + 8, :] = jnp.zeros((8, W), f32)
    for k in range(1, Z):
        w_rz(zpeers(k)).wait_recv()
    rc = pltpu.make_async_copy(reqr, reqs, l_sem.at[1])
    rc.start()
    rc.wait()
    oc.wait()
    all_sec.wait_recv()

    lowb = rb.bit_length() - 1
    left, low, first = D.bit_length() - 1, lowb, True
    while left:
        b = min(3, left)
        left -= b
        mix_pass(recv if first else table, table, rows, low, b, norm if left == 0 else None)
        low, first = low + b, False

    R = D * cap
    for x in range(X):
        def answer(z, _, x=x):
            for c in range(cap):
                ans[x, pl.ds(z * cap + c, 1), :] = table[pl.ds(jnp.clip(reqs[x, z, 0, c], 0, rows), 1), :]
            return 0
        lax.fori_loop(0, Z, answer, 0, unroll=2 if Z % 2 == 0 else 1)
        xall[col, x * Z * cap:(x + 1) * Z * cap, :] = ans[x]

    half = R // 2
    up, down = lax.rem(col + 2, C), lax.rem(col + C - 2, C)

    def c_col(s, h, t):
        ref = xall.at[s, pl.ds(h * half, half), :]
        return rcopy(ref, ref, s_col.at[s, h, t], r_col.at[s, h], c=(sib, up, down)[t])
    started = []

    def go(s, h, t):
        started.append(c_col(s, h, t))
        started[-1].start()
    ring = C > 4
    far = lax.rem(col + 4, C)
    go(col, 0, 2)
    go(col, 1, 1 if ring else 2)
    go(col, 0, 0)
    go(col, 1, 0)
    if ring:
        go(col, 1, 2)
        go(col, 0, 1)
    slots = lambda ref, z: ref.at[:, pl.ds(pl.multiple_of(z * cap, 8), cap), :]
    c_az = lambda j: rcopy(slots(ans, j), slots(ansz, mz), s_az.at[j], r_az.at[mz], row=mx * Z + j)
    w_az = lambda j: rcopy(slots(ans, j), slots(ansz, j), s_az.at[j], r_az.at[j], row=mx * Z + j)
    flat = lambda x: ret.at[pl.ds(pl.multiple_of(x * Z * cap, 8), Z * cap), :]
    c_ax = lambda j: rcopy(ansz.at[j], flat(mx), s_ax.at[j], r_ax.at[mx], row=j * Z + mz)
    w_ax = lambda j: rcopy(ansz.at[j], flat(j), s_ax.at[j], r_ax.at[j], row=j * Z + mz)
    for k in range(1, Z):
        c_az(zpeers(k)).start()
    ansz[:, pl.ds(pl.multiple_of(mz * cap, 8), cap), :] = ans[:, pl.ds(pl.multiple_of(mz * cap, 8), cap), :]

    mine = jnp.transpose(xall[col])

    def block(s):
        part[pl.ds(pl.multiple_of(s * W, W), W), :] = jnp.transpose(
            jnp.dot(mine, xall[s], precision=HI, preferred_element_type=f32))
    q = C * W // X
    xs = lambda j: part.at[pl.ds(pl.multiple_of(j * q, q), q), :]
    c_x = lambda j: rcopy(xs(j), xr.at[mx], s_x.at[j], r_x.at[mx], row=j * Z + mz)
    w_x = lambda j: rcopy(xs(j), xr.at[j], s_x.at[j], r_x.at[j], row=j * Z + mz)
    per_x = X * 2 // C
    chip = col // 2

    def along(k):
        a, b = lax.rem(col + 2 * k, C), lax.rem(sib + 2 * k, C)
        for h in range(2):
            c_col(b, h, 0).wait_recv()
        block(a)
        block(b)
        j = lax.rem(chip + k, C // 2)
        for n in range(per_x):
            @pl.when(mx != j * per_x + n)
            def _():
                c_x(j * per_x + n).start()
    if ring:
        along(0)
        c_col(up, 0, 0).wait_recv()
        go(up, 0, 2)
        go(up, 0, 0)
        c_col(down, 1, 0).wait_recv()
        go(down, 1, 1)
        go(down, 1, 0)
        c_col(up, 1, 0).wait_recv()
        go(up, 1, 0)
        c_col(down, 0, 0).wait_recv()
        go(down, 0, 0)
        along(1)
        along(3)
        for h in range(2):
            c_col(far, h, 0).wait_recv()
            go(far, h, 0)
        along(2)
    else:
        for h in range(2):
            c_col(up, h, 0).wait_recv()
            go(up, h, 0)
        along(0)
        along(1)

    xr[mx] = part[pl.ds(pl.multiple_of(mx * q, q), q), :]

    for j in xpeers:
        w_x(j).wait_recv()
    acc = xr[0]
    for j in range(1, X):
        acc = acc + xr[j]
    e = q // Z
    zs[...] = acc.reshape(Z, e, W)
    c_z = lambda j: rcopy(zs.at[j], zr.at[mz], s_z.at[j], r_z.at[mz], row=mx * Z + j)
    w_z = lambda j: rcopy(zs.at[j], zr.at[j], s_z.at[j], r_z.at[j], row=mx * Z + j)
    for k in range(1, Z):
        c_z(zpeers(k)).start()
    zr[mz] = zs[mz]
    for k in range(1, Z):
        w_az(zpeers(k)).wait_recv()
    for j in xpeers:
        c_ax(j).start()
    ret[pl.ds(pl.multiple_of(mx * Z * cap, 8), Z * cap), :] = ansz[mx]
    for k in range(1, Z):
        w_z(zpeers(k)).wait_recv()
    acc = zr[0]
    for j in range(1, Z):
        acc = acc + zr[j]
    gb[col, pl.ds(pl.multiple_of(mx * q + mz * e, e), e), :] = acc / samples
    ze = lambda j: gb.at[col, pl.ds(pl.multiple_of(mx * q + j * e, e), e), :]
    c_zg = lambda j: rcopy(ze(mz), ze(mz), s_zg.at[j], r_zg.at[mz], row=mx * Z + j)
    w_zg = lambda j: rcopy(ze(j), ze(j), s_zg.at[j], r_zg.at[j], row=mx * Z + j)
    for k in range(1, Z):
        c_zg(zpeers(k)).start()
    for k in range(1, Z):
        w_zg(zpeers(k)).wait_recv()
    per = C // X
    gblk = lambda s, p: gb.at[s, pl.ds(pl.multiple_of(p * W, W), W), :]
    c_xg = lambda p, j: rcopy(gblk(col, p), gblk(col, p), s_xg.at[p, j], r_xg.at[p], row=j * Z + mz)
    c_cg = lambda p, k: rcopy(gblk(col, p), gblk(col, p), s_cg.at[p, k], r_cg.at[col, p], c=ypeers[k])
    c_fw = lambda s, p: rcopy(gblk(s, p), gblk(s, p), s_fw.at[s, p], r_cg.at[s, p], c=sib)

    def along_x(p):
        @pl.when((mx == p // per) & (p <= col))
        def _():
            for j in xpeers:
                c_xg(p, j).start()

    def own_block(p):
        @pl.when(p <= col)
        def _():
            @pl.when(mx != p // per)
            def _():
                c_xg(p, mx).wait_recv()
            c_fw(col, p).start()
            for k in (1, 0, 2) if len(ypeers) == 3 else range(len(ypeers)):
                c_cg(p, k).start()

    def pass_on(p):
        for s in ypeers:
            @pl.when((p <= s) & (p + s > 0))
            def _():
                c_fw(s, p).wait_recv()
                c_fw(s, p).start()

    def first_block():
        @pl.when((col % 2 == 0) & (col > 0))
        def _():
            c_fw(0, 0).wait_recv()
            c_fw(0, 0).start()

        @pl.when(col % 2 == 1)
        def _():
            c_fw(0, 0).wait_recv()

    def arrived(p):
        for k in range(C // 2):
            s = lax.rem(sib + 2 * k, C)

            @pl.when((p <= s) & (p + s > 0))
            def _():
                c_fw(s, p).wait_recv()

    def each(fn, lo, hi):
        lax.fori_loop(lo, hi, lambda p, _: (fn(p), 0)[1], 0)
    each(along_x, 0, C)
    own_block(0)
    own_block(1)
    u[...] = jnp.zeros_like(u)
    all_sec.wait_send()
    for j in xpeers:
        w_rx(j).wait_send()
    for k in range(1, Z):
        w_rz(zpeers(k)).wait_send()
        w_az(zpeers(k)).wait_send()
        w_z(zpeers(k)).wait_send()
    for j in xpeers:
        w_ax(j).wait_recv()

    def keep(t, _):
        k, first = t // 16, t % 16
        for i in range(8):
            at = jnp.clip(owns[k, 0, first * 8 + i], 0, R - 1)
            sk_ref[pl.ds(t * 8 + i, 1), :] = ret[pl.ds(at, 1), :]
        return 0
    lax.fori_loop(0, S // 8, keep, 0)
    own_block(2)
    first_block()

    pr = lax.broadcasted_iota(jnp.int32, (W, W), 0)
    pc = lax.broadcasted_iota(jnp.int32, (W, W), 1)

    def panel(p, _):
        for ahead, fn in ((3, own_block), (1, pass_on)):
            @pl.when((p > 0) & (p + ahead < C))
            def _():
                fn(p + ahead)
        @pl.when(p > 0)
        def _():
            arrived(p)
        base = pl.multiple_of(p * W, W)
        for pp in range(C):
            @pl.when(p == pp)
            def _():
                a0 = pp * W
                for t in range(pp, C if pp else 1):
                    u[a0:a0 + W, t * W:(t + 1) * W] = gb[t, a0:a0 + W, :]
                if pp:
                    u[a0:a0 + W, a0:] = u[a0:a0 + W, a0:] - dot3(
                        jnp.transpose(u[0:a0, a0:a0 + W]), u[0:a0, a0:])
        aug[:, 0:W] = u[pl.ds(base, W), pl.ds(base, W)]
        aug[:, W:] = jnp.where(pr == pc, 1.0, 0.0).astype(f32)
        panel_factor(aug, upan)
        u[pl.ds(base, W), pl.ds(base, W)] = jnp.where(pr <= pc, upan[:, 0:W], 0.0)

        @pl.when(p == 0)
        def _():
            pass_on(0)
            own_block(3)
            pass_on(1)
            arrived(0)
            for t in range(1, C):
                u[0:W, t * W:(t + 1) * W] = gb[t, 0:W, :]
        for pp in range(C - 1):
            @pl.when(p == pp)
            def _():
                a0, a1 = pp * W, (pp + 1) * W
                linv = jnp.where(pr >= pc, upan[:, W:], 0.0)
                u[a0:a1, a1:] = dot3(linv, u[a0:a1, a1:])
        return 0

    lax.fori_loop(0, C, panel, 0)
    here = pl.ds(pl.multiple_of(col * W, W), W)
    for j in range(C):
        fac_ref[j * W:(j + 1) * W, :] = jnp.transpose(u[here, j * W:(j + 1) * W])

    for j in xpeers:
        w_ax(j).wait_send()
    for c in started:
        c.wait_send()
    for j in xpeers:
        w_x(j).wait_send()

    def left(p):
        @pl.when(p <= col)
        def _():
            @pl.when(mx == p // per)
            def _():
                for j in xpeers:
                    c_xg(p, j).wait_send()
            for k in range(len(ypeers)):
                c_cg(p, k).wait_send()
            c_fw(col, p).wait_send()
        for s in ypeers:
            @pl.when(p <= s)
            def _():
                c_fw(s, p).wait_send()
    each(left, 0, C)
    for k in range(1, Z):
        w_zg(zpeers(k)).wait_send()


def exchange(a, signs, blocks, offs, X, Z, C):
    rows, W = a.shape
    D = X * Z
    S = offs.shape[0]
    cap = max(2, 2 * S // D)
    rb = rows // D
    R = D * cap
    q = C * W // X
    V = pltpu.VMEM
    dma = pltpu.SemaphoreType.DMA
    return pl.pallas_call(
        functools.partial(exchange_kernel, X, Z, C, 1.0 / math.sqrt(D * rows), float(D * S)),
        out_shape=(jax.ShapeDtypeStruct((C * W, W), f32), jax.ShapeDtypeStruct((S, W), f32)),
        in_specs=[pl.BlockSpec(memory_space=pl.ANY)] * 4,
        out_specs=(pl.BlockSpec(memory_space=V), pl.BlockSpec(memory_space=V)),
        scratch_shapes=[
            V((rows, W), f32), V((rows // 128, 128), jnp.int32), V((2, S // 128, 128), jnp.int32),
            V((rows, W), f32), V((rows + 8, W), f32),
            V((X, Z, 1, 128), jnp.int32), V((X, Z, 1, 128), jnp.int32), V((X, Z, 1, 128), jnp.int32),
            pltpu.SMEM((X, Z, 1, 128), jnp.int32),
            V((S // 128, 1, 128), jnp.int32), pltpu.SMEM((S // 128, 1, 128), jnp.int32),
            V((X, Z * cap, W), f32), V((X, Z * cap, W), f32), V((R, W), f32), V((C, R, W), f32),
            V((C * W, W), f32), V((X, q, W), f32), V((Z, q // Z, W), f32), V((Z, q // Z, W), f32),
            V((C, C * W, W), f32), V((C * W, C * W), f32), V((W, 2 * W), f32), V((W, 2 * W), f32),
            dma((X,)), dma((X,)), dma((Z,)), dma((Z,)), dma((1,)), dma((1,)), dma((Z,)), dma((Z,)), dma((X,)), dma((X,)),
            dma((C, 2, 3)), dma((C, 2)), dma((X,)), dma((X,)), dma((Z,)), dma((Z,)),
            dma((Z,)), dma((Z,)), dma((C, X)), dma((C,)), dma((C, C // 2)), dma((C, C)), dma((C, C)), dma((6,)),
        ],
        compiler_params=pltpu.CompilerParams(collective_id=0, has_side_effects=True, vmem_limit_bytes=60 * 2**20),
        name="exchange",
    )(a, signs.reshape(rows // 128, 128), blocks.reshape(S // 128, 128), offs.reshape(S // 128, 128))


def solution(mesh):
    x_size, z_size, c_size = 4, mesh.shape["row"] // 4, mesh.shape["col"]

    def shards(matrix, row_signs, sample_block, sample_offset):
        factor, sketch = exchange(matrix, row_signs, sample_block, sample_offset, x_size, z_size, c_size)
        return sketch, factor

    placed = (P("row", "col"), P("row"), P("row", None), P("row"))
    return jax.shard_map(
        shards,
        mesh=mesh,
        in_specs=placed,
        out_specs=(P("row", "col"), P(None, "col")),
        check_vma=False,
    )
```

```python
import functools
import math

import jax
import jax.numpy as jnp
from jax import lax
from jax.experimental import pallas as pl
from jax.experimental.pallas import tpu as pltpu
from jax.sharding import PartitionSpec as P

f32, bf16 = jnp.float32, jnp.bfloat16
TN = (((0,), (0,)), ((), ()))
HI = lax.Precision.HIGHEST


def butterflies(v):
    n, step = len(v), 1
    while step < n:
        v = [v[i] + v[i + step] if not i & step else v[i - step] - v[i] for i in range(n)]
        step *= 2
    return v


def mix_pass(src, dst, rows, low, bits, scale=None):
    n, stride = 1 << bits, 1 << low
    tiles = stride // 8
    groups = rows // (n * stride)

    def body(t, _):
        g, j = t // tiles, t % tiles
        base = g * (n * stride) + j * 8
        v = [src[pl.ds(pl.multiple_of(base + i * stride, 8), 8), :] for i in range(n)]
        v = butterflies(v)
        for i in range(n):
            dst[pl.ds(pl.multiple_of(base + i * stride, 8), 8), :] = v[i] if scale is None else v[i] * scale
        return 0

    lax.fori_loop(0, groups * tiles, body, 0, unroll=2 if groups * tiles % 2 == 0 else 1)


PAN = 128
BLK = 16


def panel_factor(aug, upan):
    wide = 2 * PAN
    lanes = wide // PAN
    cur = [[aug[8 * r:8 * r + 8, h * PAN:(h + 1) * PAN] for h in range(lanes)] for r in range(BLK // 8)]
    nblk, sub = PAN // BLK, BLK // 8
    for t in range(nblk):
        lo = t * BLK
        last = t == nblk - 1
        C = [[jnp.broadcast_to(cur[r][0][:, lo + k:lo + k + 1], (8, PAN)) for r in range(sub)] for k in range(BLK)]
        if not last:
            nxt = aug[lo + BLK:lo + 2 * BLK, :]
            if t > 0:
                done = upan[0:lo, :]
                nxt = nxt - lax.dot_general(done[:, lo + BLK:lo + 2 * BLK], done, TN,
                                            precision=HI, preferred_element_type=f32)
            acc = [[None] * lanes for _ in range(sub)]
            N = [[jnp.broadcast_to(nxt[8 * r:8 * r + 8, lo + k:lo + k + 1], (8, PAN)) for r in range(sub)] for k in range(BLK)]
        R = cur
        for k in range(BLK):
            rs = lax.rsqrt(C[k][k // 8][k % 8:k % 8 + 1, :])
            u = [R[k // 8][h][k % 8:k % 8 + 1, :] * rs for h in range(lanes)]
            for h in range(lanes):
                upan[lo + k:lo + k + 1, h * PAN:(h + 1) * PAN] = u[h]
            first = (k + 1) // 8
            L = [C[k][r] * rs if r >= first else None for r in range(sub)]
            Nl = [N[k][r] * rs for r in range(sub)] if not last else None
            for c in range(k + 1, BLK):
                m = L[c // 8][c % 8:c % 8 + 1, :]
                for r in range(c // 8, sub):
                    C[c][r] = C[c][r] - L[r] * m
                if not last:
                    for r in range(sub):
                        N[c][r] = N[c][r] - Nl[r] * m
            for h in range(lanes):
                for r in range(first, sub):
                    R[r][h] = R[r][h] - L[r] * u[h]
                if not last:
                    for r in range(sub):
                        acc[r][h] = Nl[r] * u[h] if acc[r][h] is None else acc[r][h] + Nl[r] * u[h]
        if not last:
            cur = [[nxt[8 * r:8 * r + 8, h * PAN:(h + 1) * PAN] - acc[r][h] for h in range(lanes)] for r in range(sub)]


def split2(x):
    h = x.astype(bf16)
    return h, (x - h.astype(f32)).astype(bf16)


def dot3(a, b):
    ah, al = split2(a)
    bh, bl = split2(b)
    return jnp.dot(jnp.concatenate([ah, al], axis=1), jnp.concatenate([bh, bh], axis=0), preferred_element_type=f32) \
        + jnp.dot(ah, bl, preferred_element_type=f32)


def exchange_kernel(X, Z, C, norm, samples,
                    a_ref, sign_ref, blk_ref, off_ref,
                    fac_ref, sk_ref,
                    v, sign, pos, recv, table, req, reqx, reqr, reqs, own, owns, ans, ansz, ret, xall, part, xr, zs, zr,
                    gb, u, aug, upan,
                    s_rx, r_rx, s_rz, r_rz, s_sec, r_sec, s_az, r_az, s_ax, r_ax, s_col, r_col, s_x, r_x, s_z, r_z,
                    s_zg, r_zg, s_xg, r_xg, s_cg, s_fw, r_cg, l_sem):
    D = X * Z
    rows, W = v.shape
    rb = rows // D
    cap = ret.shape[0] // D
    SR = blk_ref.shape[0]
    S = SR * 128
    me, col = lax.axis_index("row"), lax.axis_index("col")
    mx, mz = me // Z, me % Z
    sib = col + 1 - 2 * (col % 2)

    def rcopy(src, dst, ss, rs, row=None, c=None):
        dev = {"row": row} if c is None else {"col": c}
        return pltpu.make_async_remote_copy(src_ref=src, dst_ref=dst, send_sem=ss, recv_sem=rs,
                                            device_id=dev, device_id_type=pl.DeviceIdType.MESH)

    fetch = [pltpu.make_async_copy(src, dst, l_sem.at[2 + k]) for k, (src, dst) in enumerate(
        [(blk_ref, pos.at[0]), (off_ref, pos.at[1]), (sign_ref, sign), (a_ref, v)])]
    for c in fetch:
        c.start()

    bar = pltpu.get_barrier_semaphore()

    def greet(k, _):
        pl.semaphore_signal(bar, inc=1, device_id={"row": lax.rem(me + k, D)}, device_id_type=pl.DeviceIdType.MESH)
        return 0
    lax.fori_loop(1, D, greet, 0)
    ypeers = [lax.rem(col + 2 * k, C) for k in range(1, C // 2)]
    for c in [sib] + ypeers:
        pl.semaphore_signal(bar, inc=1, device_id={"col": c}, device_id_type=pl.DeviceIdType.MESH)

    nb = rows // 128
    fetch[2].wait()
    fetch[3].wait()
    st = jnp.transpose(jnp.concatenate([sign[...].astype(f32), jnp.zeros((128 - nb, 128), f32)], axis=0))
    for j in range(nb):
        v[j * 128:(j + 1) * 128, :] = v[j * 128:(j + 1) * 128, :] * jnp.broadcast_to(st[:, j:j + 1], (128, W))

    def low_bits(g, _):
        base = pl.multiple_of(g * 64, 64)
        w = butterflies([v[pl.ds(base + k, 8, stride=8), :] for k in range(8)])
        for k in range(8):
            v[pl.ds(base + k, 8, stride=8), :] = w[k]
        return 0
    lax.fori_loop(0, rows // 64, low_bits, 0, unroll=2)
    left, low = rows.bit_length() - 1 - 3, 3
    while left:
        b = left if left <= 5 else 3
        mix_pass(v, v, rows, low, b)
        low, left = low + b, left - b

    pl.semaphore_wait(bar, D - 1 + 1 + len(ypeers))

    def peer_of(k):
        return lax.rem(me + jnp.where(k % 2 == 1, (k + 1) // 2, D - k // 2), D)

    def sends(fn, lo, hi):
        def go(k, _):
            fn(peer_of(k)).start()
            return 0
        lax.fori_loop(lo, hi, go, 0)

    xpeers = [lax.rem(mx + k, X) for k in range(1, X)]
    zpeers = lambda k: lax.rem(mz + k, Z)
    c_rx = lambda j: rcopy(req.at[j], reqx.at[mx], s_rx.at[j], r_rx.at[mx], row=j * Z + mz)
    w_rx = lambda j: rcopy(req.at[j], reqx.at[j], s_rx.at[j], r_rx.at[j], row=j * Z + mz)
    c_rz = lambda j: rcopy(reqx.at[:, j], reqr.at[:, mz], s_rz.at[j], r_rz.at[mz], row=mx * Z + j)
    w_rz = lambda j: rcopy(reqx.at[:, j], reqr.at[:, j], s_rz.at[j], r_rz.at[j], row=mx * Z + j)
    sec = lambda j: v.at[pl.ds(pl.multiple_of(j * rb, rb), rb), :]
    got = lambda j: recv.at[pl.ds(pl.multiple_of(j * rb, rb), rb), :]
    c_sec = lambda j: rcopy(sec(j), got(me), s_sec.at[0], r_sec.at[0], row=j)
    others = pl.ds(0, (D - 1) * rb)
    all_sec = rcopy(v.at[others, :], recv.at[others, :], s_sec.at[0], r_sec.at[0], row=lax.rem(me + 1, D))
    sends(c_sec, 1, D // 4)
    fetch[0].wait()
    fetch[1].wait()

    both = jnp.transpose(jnp.concatenate(
        [pos[0].astype(f32), pos[1].astype(f32), jnp.zeros((128 - 2 * SR, 128), f32)], axis=0))
    blocks, offc = [jnp.concatenate([both[:, k:k + 1] for k in range(b, b + SR)], axis=0) for b in (0, SR)]
    lane = lax.broadcasted_iota(jnp.int32, (S, 128), 1)
    onehot = (blocks == lane.astype(f32)).astype(f32)
    ri = lax.broadcasted_iota(jnp.int32, (S, S), 0)
    ci = lax.broadcasted_iota(jnp.int32, (S, S), 1)
    before = jnp.dot((ci < ri).astype(bf16), onehot.astype(bf16), preferred_element_type=f32)
    slot = jnp.sum(before * onehot, axis=1, keepdims=True)
    val = jnp.where(lane.astype(f32) == slot, offc - float(rows), 0.0)
    wanted = lax.dot_general(onehot, val, TN, precision=HI, preferred_element_type=f32) + float(rows)
    wanted = wanted.astype(jnp.int32)
    for j in range(D):
        req[j // Z, j % Z] = wanted[j:j + 1, :]
    place = blocks * float(cap) + slot
    for k in range(S // 128):
        t = jnp.transpose(jnp.broadcast_to(place[k * 128:(k + 1) * 128, :], (128, 128)))
        own[k] = t[0:1, :].astype(jnp.int32)
    oc = pltpu.make_async_copy(own, owns, l_sem.at[0])
    oc.start()

    for j in xpeers:
        c_rx(j).start()
    reqx[mx] = req[mx]
    sends(c_sec, D // 4, D // 2)
    for j in xpeers:
        w_rx(j).wait_recv()
    for k in range(1, Z):
        c_rz(zpeers(k)).start()
    sends(c_sec, D // 2, D)
    reqr[:, mz] = reqx[:, mz]
    recv[pl.ds(pl.multiple_of(me * rb, rb), rb), :] = v[pl.ds(pl.multiple_of(me * rb, rb), rb), :]
    table[rows:rows + 8, :] = jnp.zeros((8, W), f32)
    for k in range(1, Z):
        w_rz(zpeers(k)).wait_recv()
    rc = pltpu.make_async_copy(reqr, reqs, l_sem.at[1])
    rc.start()
    rc.wait()
    oc.wait()
    all_sec.wait_recv()

    lowb = rb.bit_length() - 1
    left, low, first = D.bit_length() - 1, lowb, True
    while left:
        b = min(3, left)
        left -= b
        mix_pass(recv if first else table, table, rows, low, b, norm if left == 0 else None)
        low, first = low + b, False

    R = D * cap
    for x in range(X):
        def answer(z, _, x=x):
            for c in range(cap):
                ans[x, pl.ds(z * cap + c, 1), :] = table[pl.ds(jnp.clip(reqs[x, z, 0, c], 0, rows), 1), :]
            return 0
        lax.fori_loop(0, Z, answer, 0, unroll=2 if Z % 2 == 0 else 1)
        xall[col, x * Z * cap:(x + 1) * Z * cap, :] = ans[x]

    half = R // 2
    up, down = lax.rem(col + 2, C), lax.rem(col + C - 2, C)

    def c_col(s, h, t):
        ref = xall.at[s, pl.ds(h * half, half), :]
        return rcopy(ref, ref, s_col.at[s, h, t], r_col.at[s, h], c=(sib, up, down)[t])
    started = []

    def go(s, h, t):
        started.append(c_col(s, h, t))
        started[-1].start()
    ring = C > 4
    far = lax.rem(col + 4, C)
    go(col, 0, 2)
    go(col, 1, 1 if ring else 2)
    go(col, 0, 0)
    go(col, 1, 0)
    if ring:
        go(col, 1, 2)
        go(col, 0, 1)
    slots = lambda ref, z: ref.at[:, pl.ds(pl.multiple_of(z * cap, 8), cap), :]
    c_az = lambda j: rcopy(slots(ans, j), slots(ansz, mz), s_az.at[j], r_az.at[mz], row=mx * Z + j)
    w_az = lambda j: rcopy(slots(ans, j), slots(ansz, j), s_az.at[j], r_az.at[j], row=mx * Z + j)
    flat = lambda x: ret.at[pl.ds(pl.multiple_of(x * Z * cap, 8), Z * cap), :]
    c_ax = lambda j: rcopy(ansz.at[j], flat(mx), s_ax.at[j], r_ax.at[mx], row=j * Z + mz)
    w_ax = lambda j: rcopy(ansz.at[j], flat(j), s_ax.at[j], r_ax.at[j], row=j * Z + mz)
    for k in range(1, Z):
        c_az(zpeers(k)).start()
    ansz[:, pl.ds(pl.multiple_of(mz * cap, 8), cap), :] = ans[:, pl.ds(pl.multiple_of(mz * cap, 8), cap), :]

    mine = jnp.transpose(xall[col])

    def block(s):
        part[pl.ds(pl.multiple_of(s * W, W), W), :] = jnp.transpose(
            jnp.dot(mine, xall[s], precision=HI, preferred_element_type=f32))
    q = C * W // X
    xs = lambda j: part.at[pl.ds(pl.multiple_of(j * q, q), q), :]
    c_x = lambda j: rcopy(xs(j), xr.at[mx], s_x.at[j], r_x.at[mx], row=j * Z + mz)
    w_x = lambda j: rcopy(xs(j), xr.at[j], s_x.at[j], r_x.at[j], row=j * Z + mz)
    per_x = X * 2 // C
    chip = col // 2

    def along(k):
        a, b = lax.rem(col + 2 * k, C), lax.rem(sib + 2 * k, C)
        for h in range(2):
            c_col(b, h, 0).wait_recv()
        block(a)
        block(b)
        j = lax.rem(chip + k, C // 2)
        for n in range(per_x):
            @pl.when(mx != j * per_x + n)
            def _():
                c_x(j * per_x + n).start()
    if ring:
        along(0)
        c_col(up, 0, 0).wait_recv()
        go(up, 0, 2)
        go(up, 0, 0)
        c_col(down, 1, 0).wait_recv()
        go(down, 1, 1)
        go(down, 1, 0)
        c_col(up, 1, 0).wait_recv()
        go(up, 1, 0)
        c_col(down, 0, 0).wait_recv()
        go(down, 0, 0)
        along(1)
        along(3)
        for h in range(2):
            c_col(far, h, 0).wait_recv()
            go(far, h, 0)
        along(2)
    else:
        for h in range(2):
            c_col(up, h, 0).wait_recv()
            go(up, h, 0)
        along(0)
        along(1)

    xr[mx] = part[pl.ds(pl.multiple_of(mx * q, q), q), :]

    for j in xpeers:
        w_x(j).wait_recv()
    acc = xr[0]
    for j in range(1, X):
        acc = acc + xr[j]
    e = q // Z
    zs[...] = acc.reshape(Z, e, W)
    c_z = lambda j: rcopy(zs.at[j], zr.at[mz], s_z.at[j], r_z.at[mz], row=mx * Z + j)
    w_z = lambda j: rcopy(zs.at[j], zr.at[j], s_z.at[j], r_z.at[j], row=mx * Z + j)
    for k in range(1, Z):
        c_z(zpeers(k)).start()
    zr[mz] = zs[mz]
    for k in range(1, Z):
        w_az(zpeers(k)).wait_recv()
    for j in xpeers:
        c_ax(j).start()
    ret[pl.ds(pl.multiple_of(mx * Z * cap, 8), Z * cap), :] = ansz[mx]
    for k in range(1, Z):
        w_z(zpeers(k)).wait_recv()
    acc = zr[0]
    for j in range(1, Z):
        acc = acc + zr[j]
    gb[col, pl.ds(pl.multiple_of(mx * q + mz * e, e), e), :] = acc / samples
    ze = lambda j: gb.at[col, pl.ds(pl.multiple_of(mx * q + j * e, e), e), :]
    c_zg = lambda j: rcopy(ze(mz), ze(mz), s_zg.at[j], r_zg.at[mz], row=mx * Z + j)
    w_zg = lambda j: rcopy(ze(j), ze(j), s_zg.at[j], r_zg.at[j], row=mx * Z + j)
    for k in range(1, Z):
        c_zg(zpeers(k)).start()
    for k in range(1, Z):
        w_zg(zpeers(k)).wait_recv()
    per = C // X
    gblk = lambda s, p: gb.at[s, pl.ds(pl.multiple_of(p * W, W), W), :]
    c_xg = lambda p, j: rcopy(gblk(col, p), gblk(col, p), s_xg.at[p, j], r_xg.at[p], row=j * Z + mz)
    c_cg = lambda p, k: rcopy(gblk(col, p), gblk(col, p), s_cg.at[p, k], r_cg.at[col, p], c=ypeers[k])
    c_fw = lambda s, p: rcopy(gblk(s, p), gblk(s, p), s_fw.at[s, p], r_cg.at[s, p], c=sib)

    def along_x(p):
        @pl.when((mx == p // per) & (p <= col))
        def _():
            for j in xpeers:
                c_xg(p, j).start()

    def own_block(p):
        @pl.when(p <= col)
        def _():
            @pl.when(mx != p // per)
            def _():
                c_xg(p, mx).wait_recv()
            c_fw(col, p).start()
            for k in (1, 0, 2) if len(ypeers) == 3 else range(len(ypeers)):
                c_cg(p, k).start()

    def pass_on(p):
        for s in ypeers:
            @pl.when((p <= s) & (p + s > 0))
            def _():
                c_fw(s, p).wait_recv()
                c_fw(s, p).start()

    def first_block():
        @pl.when((col % 2 == 0) & (col > 0))
        def _():
            c_fw(0, 0).wait_recv()
            c_fw(0, 0).start()

        @pl.when(col % 2 == 1)
        def _():
            c_fw(0, 0).wait_recv()

    def arrived(p):
        for k in range(C // 2):
            s = lax.rem(sib + 2 * k, C)

            @pl.when((p <= s) & (p + s > 0))
            def _():
                c_fw(s, p).wait_recv()

    def each(fn, lo, hi):
        lax.fori_loop(lo, hi, lambda p, _: (fn(p), 0)[1], 0)
    each(along_x, 0, C)
    own_block(0)
    own_block(1)
    u[...] = jnp.zeros_like(u)
    all_sec.wait_send()
    for j in xpeers:
        w_rx(j).wait_send()
    for k in range(1, Z):
        w_rz(zpeers(k)).wait_send()
        w_az(zpeers(k)).wait_send()
        w_z(zpeers(k)).wait_send()
    for j in xpeers:
        w_ax(j).wait_recv()

    def keep(t, _):
        k, first = t // 16, t % 16
        for i in range(8):
            at = jnp.clip(owns[k, 0, first * 8 + i], 0, R - 1)
            sk_ref[pl.ds(t * 8 + i, 1), :] = ret[pl.ds(at, 1), :]
        return 0
    lax.fori_loop(0, S // 8, keep, 0)
    own_block(2)
    first_block()

    pr = lax.broadcasted_iota(jnp.int32, (W, W), 0)
    pc = lax.broadcasted_iota(jnp.int32, (W, W), 1)

    def panel(p, _):
        for ahead, fn in ((3, own_block), (1, pass_on)):
            @pl.when((p > 0) & (p + ahead < C))
            def _():
                fn(p + ahead)
        @pl.when(p > 0)
        def _():
            arrived(p)
        base = pl.multiple_of(p * W, W)
        for pp in range(C):
            @pl.when(p == pp)
            def _():
                a0 = pp * W
                for t in range(pp, C if pp else 1):
                    u[a0:a0 + W, t * W:(t + 1) * W] = gb[t, a0:a0 + W, :]
                if pp:
                    u[a0:a0 + W, a0:] = u[a0:a0 + W, a0:] - dot3(
                        jnp.transpose(u[0:a0, a0:a0 + W]), u[0:a0, a0:])
        aug[:, 0:W] = u[pl.ds(base, W), pl.ds(base, W)]
        aug[:, W:] = jnp.where(pr == pc, 1.0, 0.0).astype(f32)
        panel_factor(aug, upan)
        u[pl.ds(base, W), pl.ds(base, W)] = jnp.where(pr <= pc, upan[:, 0:W], 0.0)

        @pl.when(p == 0)
        def _():
            pass_on(0)
            own_block(3)
            pass_on(1)
            arrived(0)
            for t in range(1, C):
                u[0:W, t * W:(t + 1) * W] = gb[t, 0:W, :]
        for pp in range(C - 1):
            @pl.when(p == pp)
            def _():
                a0, a1 = pp * W, (pp + 1) * W
                linv = jnp.where(pr >= pc, upan[:, W:], 0.0)
                u[a0:a1, a1:] = dot3(linv, u[a0:a1, a1:])
        return 0

    lax.fori_loop(0, C, panel, 0)
    here = pl.ds(pl.multiple_of(col * W, W), W)
    for j in range(C):
        fac_ref[j * W:(j + 1) * W, :] = jnp.transpose(u[here, j * W:(j + 1) * W])

    for j in xpeers:
        w_ax(j).wait_send()
    for c in started:
        c.wait_send()
    for j in xpeers:
        w_x(j).wait_send()

    def left(p):
        @pl.when(p <= col)
        def _():
            @pl.when(mx == p // per)
            def _():
                for j in xpeers:
                    c_xg(p, j).wait_send()
            for k in range(len(ypeers)):
                c_cg(p, k).wait_send()
            c_fw(col, p).wait_send()
        for s in ypeers:
            @pl.when(p <= s)
            def _():
                c_fw(s, p).wait_send()
    each(left, 0, C)
    for k in range(1, Z):
        w_zg(zpeers(k)).wait_send()


def exchange(a, signs, blocks, offs, X, Z, C):
    rows, W = a.shape
    D = X * Z
    S = offs.shape[0]
    cap = max(2, 2 * S // D)
    rb = rows // D
    R = D * cap
    q = C * W // X
    V = pltpu.VMEM
    dma = pltpu.SemaphoreType.DMA
    return pl.pallas_call(
        functools.partial(exchange_kernel, X, Z, C, 1.0 / math.sqrt(D * rows), float(D * S)),
        out_shape=(jax.ShapeDtypeStruct((C * W, W), f32), jax.ShapeDtypeStruct((S, W), f32)),
        in_specs=[pl.BlockSpec(memory_space=pl.ANY)] * 4,
        out_specs=(pl.BlockSpec(memory_space=V), pl.BlockSpec(memory_space=V)),
        scratch_shapes=[
            V((rows, W), f32), V((rows // 128, 128), jnp.int32), V((2, S // 128, 128), jnp.int32),
            V((rows, W), f32), V((rows + 8, W), f32),
            V((X, Z, 1, 128), jnp.int32), V((X, Z, 1, 128), jnp.int32), V((X, Z, 1, 128), jnp.int32),
            pltpu.SMEM((X, Z, 1, 128), jnp.int32),
            V((S // 128, 1, 128), jnp.int32), pltpu.SMEM((S // 128, 1, 128), jnp.int32),
            V((X, Z * cap, W), f32), V((X, Z * cap, W), f32), V((R, W), f32), V((C, R, W), f32),
            V((C * W, W), f32), V((X, q, W), f32), V((Z, q // Z, W), f32), V((Z, q // Z, W), f32),
            V((C, C * W, W), f32), V((C * W, C * W), f32), V((W, 2 * W), f32), V((W, 2 * W), f32),
            dma((X,)), dma((X,)), dma((Z,)), dma((Z,)), dma((1,)), dma((1,)), dma((Z,)), dma((Z,)), dma((X,)), dma((X,)),
            dma((C, 2, 3)), dma((C, 2)), dma((X,)), dma((X,)), dma((Z,)), dma((Z,)),
            dma((Z,)), dma((Z,)), dma((C, X)), dma((C,)), dma((C, C // 2)), dma((C, C)), dma((C, C)), dma((6,)),
        ],
        compiler_params=pltpu.CompilerParams(collective_id=0, has_side_effects=True, vmem_limit_bytes=60 * 2**20),
        name="exchange",
    )(a, signs.reshape(rows // 128, 128), blocks.reshape(S // 128, 128), offs.reshape(S // 128, 128))


def solution(mesh):
    x_size, z_size, c_size = 4, mesh.shape["row"] // 4, mesh.shape["col"]

    def shards(matrix, row_signs, sample_block, sample_offset):
        factor, sketch = exchange(matrix, row_signs, sample_block, sample_offset, x_size, z_size, c_size)
        return sketch, factor

    placed = (P("row", "col"), P("row"), P("row", None), P("row"))
    return jax.shard_map(
        shards,
        mesh=mesh,
        in_specs=placed,
        out_specs=(P("row", "col"), P(None, "col")),
        check_vma=False,
    )
```
